256 devices in a mesh: patch: 64 (over z, y, core), sample: 4 (over x).
Axes of the slice: x: 4, y: 4, z: 8, core: 2. Of those that a mesh axis runs over, the one named last changes fastest.
Arguments:
- features: bfloat16 [4, 32768, 512], P('sample', 'patch'), may hold values from -600 to 600
- cotangent: bfloat16 [4, 32768, 512], P('sample', 'patch'), may hold values from -6 to 6
- weight_qkv: bfloat16 [512, 1536], replicated, may hold values from -5 to 5
- weight_out: bfloat16 [512, 512], replicated, may hold values from -0.25 to 0.25
- key_tiles: int32 [256, 8], replicated, may hold values from 0 to 255, as said below
- tile_valid: int32 [256, 8], replicated, may hold values from 0 to 1, as said below
Outputs:
- grad_features: bfloat16 [4, 32768, 512], P('sample', 'patch')
- grad_qkv: float32 [512, 1536], replicated
- grad_out: float32 [512, 512], replicated
The draws below stay inside these ranges and needn't reach their ends.
Inputs may be any that keep to these rules, and one draw needn't show every extreme that they name: `key_tiles`: row g names 8 distinct tile ids. A tile's patch is its id // 4. The first id is g itself, the next 3 are other tiles of g's patch, and the last 4 lie one each in the patches at offsets -2 to 2 other than 0 around the cycle of patches, in rising order of offset. Over the rows of one patch exactly 2 distinct tiles of each such neighbouring patch are named. `tile_valid`: column 0 is always 1.
All inputs are finite; a program needn't handle non-finite values.
Results may differ from the reference program's by a relative error of at most 0.0088.
Values may be sent and summed in bfloat16 or wider, within the bound.
A program may use at most 192 MiB of HBM per device.

```python
import jax
import jax.numpy as jnp
from jax import lax

D = 512
HEADS = 4
TILE = 128
TILE_DEV = 4
NB = 8
REACH = 2
CAP = 2
SAMPLES = 4
TILES = 256
NODES = 32768


def draw_features(key, part):
    base = jnp.clip(jax.random.normal(jax.random.fold_in(key, 1), (SAMPLES, NODES, D), jnp.float32), -5.0, 5.0)
    return base.astype(jnp.bfloat16)


def draw_weight_qkv(key, part):
    first = jnp.clip(jax.random.normal(jax.random.fold_in(key, 5), (D, 3 * D), jnp.float32), -5.0, 5.0)
    return (first * D ** (-0.5)).astype(jnp.bfloat16)


def draw_key_tiles(key, part):
    patches = TILES // TILE_DEV
    patch_of = jnp.arange(TILES, dtype=jnp.int32) // TILE_DEV
    local = jnp.arange(TILES, dtype=jnp.int32) % TILE_DEV
    own_keys = jax.random.split(jax.random.fold_in(key, 11), TILES)
    others = jax.vmap(lambda single: jax.random.permutation(single, TILE_DEV - 1))(own_keys)[:, :NB - 1 - 2 * REACH]
    neighbours = (local[:, None] + 1 + others.astype(jnp.int32)) % TILE_DEV + patch_of[:, None] * TILE_DEV
    columns = [(patch_of * TILE_DEV + local)[:, None], neighbours]
    chosen_keys = jax.random.split(jax.random.fold_in(key, 12), patches * 2 * REACH)
    chosen = jax.vmap(lambda single: jax.random.permutation(single, TILE_DEV)[:CAP])(chosen_keys)
    chosen = chosen.astype(jnp.int32).reshape(patches, 2 * REACH, CAP)
    picked = jax.random.randint(jax.random.fold_in(key, 13), (TILES, 2 * REACH), 0, CAP, jnp.int32)
    picked = jnp.where(local[:, None] < CAP, local[:, None], picked)
    offsets = [shift_by for shift_by in range(-REACH, REACH + 1) if shift_by != 0]
    for offset_index, shift_by in enumerate(offsets):
        target = (patch_of + shift_by) % patches
        entry = chosen[patch_of, offset_index, picked[:, offset_index]]
        columns.append((target * TILE_DEV + entry)[:, None])
    return jnp.concatenate(columns, 1).astype(jnp.int32)


def draw_tile_valid(key, part):
    levels = jax.random.randint(jax.random.fold_in(key, 21), (TILES, NB), 0, 4, jnp.int32)
    flags = (levels > 0).astype(jnp.int32)
    return flags.at[:, 0].set(1)


def block_levels(stream_key, dims, shards, least, largest):
    def one(position, shards_of):
        steps = jax.random.uniform(jax.random.fold_in(jax.random.fold_in(stream_key, 6), position), (shards_of,), jnp.float32, least / len(shards), largest / len(shards))
        return jnp.repeat(jnp.exp(steps), dims[position] // shards_of).reshape((-1,) + (1,) * (len(dims) - position - 1))

    level = one(*shards[0])
    for cut in shards[1:]:
        level = level * one(*cut)
    return level


def noise(rng, dims, spread, reach, cuts=(), kind=jnp.bfloat16):
    entries = jax.random.normal(rng, dims, jnp.float32) * spread
    if len(cuts) > 0:
        entries = block_levels(rng, dims, cuts, -0.22, 0.18) * entries
    return jnp.clip(entries, min=-reach, max=reach).astype(kind)


def setup_inputs(seed: int = 0) -> dict:
    keys = jax.random.split(jax.random.key(seed), 7)
    features = draw_features(jax.random.fold_in(keys[6], 71), 0)
    cotangent = noise(keys[1], (SAMPLES, NODES, D), 1.0, 6.0, ((0, 4), (1, 64)))
    weight_qkv = draw_weight_qkv(jax.random.fold_in(keys[6], 71), 0)
    weight_out = noise(keys[3], (D, D), D ** -0.5, 0.25)
    key_tiles = draw_key_tiles(jax.random.fold_in(keys[6], 71), 0)
    tile_valid = draw_tile_valid(jax.random.fold_in(keys[6], 71), 0)
    return dict(features=features, cotangent=cotangent, weight_qkv=weight_qkv, weight_out=weight_out, key_tiles=key_tiles, tile_valid=tile_valid)


epsilon = 1e-06

def tile_backward(query_tile, pair_tiles, live_flags, grad_tile):
    row_count = query_tile.shape[0]
    model_width = query_tile.shape[1]
    head_width = model_width // HEADS
    scaling = head_width ** (-0.5)
    key_heads = pair_tiles[:, :, :model_width].reshape(-1, HEADS, head_width).astype(jnp.float32)
    value_heads = pair_tiles[:, :, model_width:].reshape(-1, HEADS, head_width).astype(jnp.float32)
    query_heads = query_tile.reshape(row_count, HEADS, head_width).astype(jnp.float32)
    grad_heads = grad_tile.reshape(row_count, HEADS, head_width).astype(jnp.float32)
    scores = jnp.einsum('qhd,khd->hqk', query_heads, key_heads) * scaling
    live_mask = jnp.repeat(live_flags > 0, pair_tiles.shape[1])
    scores = jnp.where(live_mask[None, None, :], scores, -jnp.inf)
    highest = lax.optimization_barrier(jnp.max(scores, -1, keepdims=True))
    expanded = jnp.exp(scores - highest)
    attention = expanded / lax.optimization_barrier(jnp.sum(expanded, -1, keepdims=True))
    attention_low = lax.optimization_barrier(attention.astype(jnp.bfloat16)).astype(jnp.float32)
    attended = jnp.einsum('hqk,khd->qhd', attention_low, value_heads).astype(jnp.bfloat16).reshape(row_count, model_width)
    dprob = jnp.einsum('qhd,khd->hqk', grad_heads, value_heads)
    centre = lax.optimization_barrier(jnp.sum(attention * dprob, -1, keepdims=True))
    dscore = lax.optimization_barrier((attention * (dprob - centre) * scaling).astype(jnp.bfloat16)).astype(jnp.float32)
    dquery = jnp.einsum('hqk,khd->qhd', dscore, key_heads).reshape(row_count, model_width)
    dkey = jnp.einsum('hqk,qhd->khd', dscore, query_heads).reshape(pair_tiles.shape[0], pair_tiles.shape[1], model_width)
    dvalue = jnp.einsum('hqk,qhd->khd', attention_low, grad_heads).reshape(pair_tiles.shape[0], pair_tiles.shape[1], model_width)
    return (attended, dquery, jnp.concatenate([dkey, dvalue], -1))

def reference(features, cotangent, weight_qkv, weight_out, key_tiles, tile_valid):
    factor = float(SAMPLES * NODES) ** (-0.5)
    total_qkv = jnp.zeros((D, 3 * D), jnp.float32)
    total_out = jnp.zeros((D, D), jnp.float32)
    results = []
    for sample in range(SAMPLES):
        inputs = features[sample].astype(jnp.float32)
        inverse = lax.rsqrt(lax.optimization_barrier(jnp.mean(inputs * inputs, -1, keepdims=True)) + epsilon)
        normed = inputs * inverse
        normed_low = normed.astype(jnp.bfloat16)
        projected = jnp.dot(normed_low, weight_qkv, preferred_element_type=jnp.float32).astype(jnp.bfloat16)
        queries = projected[:, :D].reshape(TILES, TILE, D)
        pair_all = projected[:, D:].reshape(TILES, TILE, 2 * D)
        grad_rows = cotangent[sample]
        grad_attended = jnp.dot(grad_rows, weight_out.T, preferred_element_type=jnp.float32).astype(jnp.bfloat16)
        grad_tiles = grad_attended.reshape(TILES, TILE, D)

        def advance(running, pieces):
            query_tile, slot_ids, live_flags, grad_tile = pieces
            attended, dquery, dpairs = tile_backward(query_tile, pair_all[slot_ids], live_flags, grad_tile)
            return (running.at[slot_ids].add(dpairs), (attended, dquery))
        start_sums = jnp.zeros((TILES, TILE, 2 * D), jnp.float32)
        totals, (attended_all, dquery_all) = lax.scan(advance, start_sums, (queries, key_tiles, tile_valid, grad_tiles))
        attended_rows = attended_all.reshape(NODES, D)
        grad_projected = jnp.concatenate([dquery_all.reshape(NODES, D), totals.reshape(NODES, 2 * D)], 1).astype(jnp.bfloat16)
        grad_normed = jnp.dot(grad_projected, weight_qkv.T, preferred_element_type=jnp.float32)
        grad_inputs = grad_rows.astype(jnp.float32) + inverse * (grad_normed - normed * lax.optimization_barrier(jnp.mean(grad_normed * normed, -1, keepdims=True)))
        results.append(grad_inputs.astype(jnp.bfloat16))
        total_qkv = total_qkv + jnp.dot(normed_low.T, grad_projected, preferred_element_type=jnp.float32)
        total_out = total_out + jnp.dot(attended_rows.T, grad_rows, preferred_element_type=jnp.float32)
    return (jnp.stack(results, 0), total_qkv * factor, total_out * factor)
```

```python
import functools

import jax
import jax.numpy as jnp
from jax import lax
from jax.experimental import pallas as pl
from jax.experimental.pallas import tpu as pltpu
from jax.sharding import PartitionSpec as P

HEADS = 4
TILE = 128
LOCAL = 4
REACH = 2
OFFSETS = [-2, -1, 1, 2]
CHIPS_Y = 4
EPS = 1e-06
MESH = pl.DeviceIdType.MESH
F32 = jnp.float32
BF16 = jnp.bfloat16
LOG2E = 1.4426950408889634

ROWS = LOCAL * TILE
HALO = 2 * TILE
ALL = ROWS + len(OFFSETS) * HALO
D = 512
HW = D // HEADS


def nn(a, b):
    return lax.dot_general(a, b, (((1,), (0,)), ((), ())), preferred_element_type=F32)


def nt(a, b):
    return lax.dot_general(a, b, (((1,), (1,)), ((), ())), preferred_element_type=F32)


def tt(a, b):
    return lax.dot_general(a, b, (((0,), (1,)), ((), ())), preferred_element_type=F32)


def tn(a, b):
    return lax.dot_general(a, b, (((0,), (0,)), ((), ())), preferred_element_type=F32)


def normalise(rows):
    wide = rows.astype(F32)
    inverse = lax.rsqrt(jnp.mean(wide * wide, -1, keepdims=True) + EPS)
    return wide, inverse


def kernel(
    dims,
    kt,
    tv,
    x_ref,
    c_ref,
    w_ref,
    wo_ref,
    gf_ref,
    out_ref,
    stage,
    halo,
    normed_t,
    q,
    k,
    v,
    ga,
    q_t,
    ga_t,
    bias,
    prob,
    dscore,
    attended,
    dquery,
    dkv_t,
    back_out,
    back_in,
    local,
    got0,
    sum0,
    got1,
    sum1,
    got2,
    got3,
    res,
    halo_send,
    halo_recv,
    back_send,
    back_recv,
    red_send,
    red_recv,
    out_sem,
):
    patches, nz, ny, nx = dims
    p = lax.axis_index("patch")
    sx = lax.axis_index("sample")
    core = lax.rem(p, 2)
    y = lax.rem(lax.div(p, 2), ny)
    z = lax.div(p, 2 * ny)

    def patch_at(zz, yy):
        return (zz * ny + yy) * 2 + core

    def first(j):
        return (
            patch_at(z, lax.rem(y + j * core, ny)),
            lax.rem(sx + j * (1 - core), nx),
        )

    def second(j):
        return (
            patch_at(z, lax.rem(y + j * (1 - core), ny)),
            lax.rem(sx + j * core, nx),
        )

    def along_z(j):
        return (patch_at(lax.rem(z + j, nz), y), sx)

    pair = (p + 1 - 2 * core, sx)
    m1 = sx * (1 - core) + y * core
    m2 = sx * core + y * (1 - core)
    group = nx

    barrier = pltpu.get_barrier_semaphore()
    greeted = (
        [(lax.rem(p + o + patches, patches), sx) for o in OFFSETS]
        + [pair]
        + [first(j) for j in range(1, group)]
        + [second(j) for j in range(1, group)]
        + [along_z(j) for j in range(1, nz)]
    )
    for device in greeted:
        pl.semaphore_signal(barrier, inc=1, device_id=device, device_id_type=MESH)

    named = []
    for oi, o in enumerate(OFFSETS):
        row = lax.rem(p - o + patches, patches) * LOCAL
        one = kt[row, LOCAL + oi]
        two = one
        for r in range(1, LOCAL):
            entry = kt[row + r, LOCAL + oi]
            two = jnp.where(entry != one, entry, two)
        named.append((one - p * LOCAL, two - p * LOCAL))
        for s in range(2):
            tile = x_ref[0, 0:TILE, :]
            for r in range(1, LOCAL):
                tile = jnp.where(named[oi][s] == r, x_ref[0, r * TILE : (r + 1) * TILE, :], tile)
            stage[oi, s * TILE : (s + 1) * TILE, :] = tile

    pl.semaphore_wait(barrier, len(greeted))

    def halo_copy(oi):
        return pltpu.make_async_remote_copy(
            src_ref=stage.at[oi],
            dst_ref=halo.at[oi],
            send_sem=halo_send.at[oi],
            recv_sem=halo_recv.at[oi],
            device_id=(lax.rem(p - OFFSETS[oi] + patches, patches), sx),
            device_id_type=MESH,
        )

    def back_copy(oi):
        return pltpu.make_async_remote_copy(
            src_ref=back_out.at[oi],
            dst_ref=back_in.at[oi],
            send_sem=back_send.at[oi],
            recv_sem=back_recv.at[oi],
            device_id=(lax.rem(p + OFFSETS[oi] + patches, patches), sx),
            device_id_type=MESH,
        )

    for oi in (0, 3, 1, 2):
        halo_copy(oi).start()

    base = p * LOCAL
    pick = []
    for t in range(LOCAL):
        pick.append(
            [
                jnp.where(kt[base + t, LOCAL + n] != kt[base, LOCAL + n], 1, 0)
                for n in range(len(OFFSETS))
            ]
        )
        for r in range(LOCAL):
            flag = jnp.int32(0)
            for j in range(LOCAL):
                flag = flag + jnp.where(kt[base + t, j] == base + r, tv[base + t, j], 0)
            low = jnp.where(flag > 0, jnp.float32(0.0), jnp.float32(-1e30))
            bias[t, :, r * TILE : (r + 1) * TILE] = jnp.full((8, TILE), low, F32)
        for n in range(len(OFFSETS)):
            flag = tv[base + t, LOCAL + n]
            low = jnp.where(flag > 0, jnp.float32(0.0), jnp.float32(-1e30))
            bias[t, :, ROWS + n * TILE : ROWS + (n + 1) * TILE] = jnp.full((8, TILE), low, F32)

    wide, inverse = normalise(x_ref[0])
    low = (wide * inverse).astype(BF16)
    normed_t[:, 0:ROWS] = low.T
    for part, target in ((0, q), (1, k), (2, v)):
        for half in range(2):
            at = part * D + half * 2 * HW
            got = nn(low, w_ref[:, at : at + 2 * HW]).astype(BF16)
            for i in range(2):
                piece = got[:, i * HW : (i + 1) * HW]
                target[half * 2 + i, 0:ROWS, :] = piece
                if part == 0:
                    q_t[half * 2 + i] = piece.T
    for half in range(2):
        at = half * 2 * HW
        got = nt(c_ref[0], wo_ref[at : at + 2 * HW, :]).astype(BF16)
        for i in range(2):
            piece = got[:, i * HW : (i + 1) * HW]
            ga[half * 2 + i] = piece
            ga_t[half * 2 + i] = piece.T

    for oi in range(len(OFFSETS)):
        halo_copy(oi).wait_recv()
        wide, inverse = normalise(halo[oi])
        low = (wide * inverse).astype(BF16)
        at_row = ROWS + oi * HALO
        normed_t[:, at_row : at_row + HALO] = low.T
        for part, target in ((1, k), (2, v)):
            for half in range(2):
                at = part * D + half * 2 * HW
                got = nn(low, w_ref[:, at : at + 2 * HW]).astype(BF16)
                for i in range(2):
                    target[half * 2 + i, at_row : at_row + HALO, :] = got[:, i * HW : (i + 1) * HW]

    half_rows = D // 2
    piece1 = half_rows // group
    piece2 = piece1 // group
    base_row = core * half_rows

    def move(h, index, src, dst, device):
        return pltpu.make_async_remote_copy(
            src_ref=src,
            dst_ref=dst,
            send_sem=red_send.at[h, index],
            recv_sem=red_recv.at[h, index],
            device_id=device,
            device_id_type=MESH,
        )

    def rows_at(start, size):
        return pl.ds(pl.multiple_of(start, 16), size)

    at1 = base_row + m1 * piece1
    at2 = at1 + m2 * piece2
    n1 = group - 1
    first_z = 1 + 2 * n1

    def copies(h, phase):
        if phase == 0:
            src = local.at[h, rows_at((1 - core) * half_rows, half_rows), :]
            return [move(h, 0, src, got0.at[h], pair)]
        if phase == 1:
            return [
                move(
                    h,
                    j,
                    sum0.at[h, rows_at(lax.rem(m1 + j, group) * piece1, piece1), :],
                    got1.at[h, j - 1],
                    first(j),
                )
                for j in range(1, group)
            ]
        if phase == 2:
            return [
                move(
                    h,
                    n1 + j,
                    sum1.at[h, rows_at(lax.rem(m2 + j, group) * piece2, piece2), :],
                    got2.at[h, j - 1],
                    second(j),
                )
                for j in range(1, group)
            ]
        if phase == 3:
            mine = got3.at[h, z]
            return [move(h, first_z + j - 1, mine, mine, along_z(j)) for j in range(1, nz)]
        if phase == 4:
            mine = res.at[h, rows_at(at2, piece2), :]
            return [
                move(h, first_z + nz - 2 + j, mine, mine, second(j)) for j in range(1, group)
            ]
        if phase == 5:
            mine = res.at[h, rows_at(at1, piece1), :]
            return [
                move(h, first_z + nz - 2 + n1 + j, mine, mine, first(j))
                for j in range(1, group)
            ]
        mine = res.at[h, rows_at(base_row, half_rows), :]
        return [move(h, first_z + nz - 2 + 2 * n1 + 1, mine, mine, pair)]

    def start(h, phase):
        for copy in copies(h, phase):
            copy.start()

    def advance(h, phase):
        for copy in copies(h, phase):
            copy.wait_recv()
        if phase == 0:
            mine = local[h, rows_at(base_row, half_rows), :].astype(F32)
            sum0[h] = (mine + got0[h].astype(F32)).astype(BF16)
        if phase == 1:
            total = sum0[h, rows_at(m1 * piece1, piece1), :].astype(F32)
            for j in range(group - 1):
                total = total + got1[h, j].astype(F32)
            sum1[h] = total.astype(BF16)
        if phase == 2:
            total = sum1[h, rows_at(m2 * piece2, piece2), :].astype(F32)
            for j in range(group - 1):
                total = total + got2[h, j].astype(F32)
            got3[h, z] = total.astype(BF16)
        if phase == 3:
            total = got3[h, 0].astype(F32)
            for j in range(1, nz):
                total = total + got3[h, j].astype(F32)
            res[h, rows_at(at2, piece2), :] = total.astype(BF16)
        if phase < 6:
            start(h, phase + 1)

    scaling = HW ** (-0.5)

    def head(h, carry):
        for t in range(LOCAL):
            rows = slice(t * TILE, (t + 1) * TILE)

            def chosen(ref):
                parts = [ref[h, 0:ROWS, :]]
                for n in range(len(OFFSETS)):
                    at = ROWS + n * HALO
                    near = ref[h, at : at + TILE, :]
                    far = ref[h, at + TILE : at + HALO, :]
                    parts.append(jnp.where(pick[t][n] == 0, near, far))
                return jnp.concatenate(parts, 0)

            keys = chosen(k)
            values = chosen(v)
            scores = nt(q[h, rows, :], keys) + bias[t, 0:1, :]
            highest = jnp.max(scores, -1, keepdims=True)
            expanded = jnp.exp2((scores - highest) * (scaling * LOG2E))
            attention = expanded * (1.0 / jnp.sum(expanded, -1, keepdims=True))
            attention_low = attention.astype(BF16)
            dprob = nt(ga[h, rows, :], values)
            centre = jnp.sum(attention * dprob, -1, keepdims=True)
            ds = (attention * (dprob - centre) * scaling).astype(BF16)
            attended[h, rows, :] = nn(attention_low, values).astype(BF16)
            dquery[h, rows, :] = nn(ds, keys).astype(BF16)
            for full, piece in ((prob, attention_low), (dscore, ds)):
                full[rows, 0:ROWS] = piece[:, 0:ROWS]
                for n in range(len(OFFSETS)):
                    part = piece[:, ROWS + n * TILE : ROWS + (n + 1) * TILE]
                    for s in range(2):
                        at = ROWS + (2 * n + s) * TILE
                        keep = jnp.where(pick[t][n] == s, 1.0, 0.0).astype(BF16)
                        full[rows, at : at + TILE] = part * keep

            @pl.when(h >= 1)
            def _():
                advance(h - 1, t)

            if t < 2:

                @pl.when(h >= 2)
                def _():
                    advance(h - 2, 4 + t)

        at = pl.multiple_of(h * HW, HW)
        dk = nn(q_t[h], dscore[...]).astype(BF16)
        dv = nn(ga_t[h], prob[...]).astype(BF16)
        dkv_t[pl.ds(at, HW), :] = dk
        dkv_t[pl.ds(pl.multiple_of(D + h * HW, HW), HW), :] = dv
        local[h, :, 0:HW] = nn(normed_t[:, 0:ROWS], dquery[h]).astype(BF16)
        local[h, :, HW : 2 * HW] = nt(normed_t[...], dk).astype(BF16)
        local[h, :, 2 * HW : 3 * HW] = nt(normed_t[...], dv).astype(BF16)
        outer = tn(attended[h], c_ref[0]).astype(BF16)
        for r in range(D // HW):
            local[h, r * HW : (r + 1) * HW, 3 * HW :] = outer[:, r * HW : (r + 1) * HW]
        start(h, 0)
        return carry

    lax.fori_loop(0, HEADS, head, 0)

    def give_back(oi):
        at = ROWS + oi * HALO
        back_out[oi] = tt(dkv_t[:, at : at + HALO], w_ref[:, D:]).astype(BF16)
        back_copy(oi).start()

    last = HEADS - 1
    advance(last - 1, 4)
    give_back(0)
    give_back(3)
    advance(last, 0)
    give_back(1)
    give_back(2)
    advance(last, 1)
    advance(last - 1, 5)
    grad = tt(dkv_t[:, 0:ROWS], w_ref[:, D:])
    for h in range(HEADS):
        grad = grad + nt(dquery[h], w_ref[:, h * HW : (h + 1) * HW])
    advance(last, 2)

    def out_copy(h):
        return pltpu.make_async_copy(res.at[h], out_ref.at[h], out_sem.at[h])

    for h in range(HEADS - 1):
        advance(h, 6)
        out_copy(h).start()
    advance(last, 3)
    for oi in range(len(OFFSETS)):
        back_copy(oi).wait_recv()
    advance(last, 4)
    for r in range(LOCAL):
        rows = slice(r * TILE, (r + 1) * TILE)
        total = grad[rows]
        for oi in range(len(OFFSETS)):
            for s in range(2):
                came = back_in[oi, s * TILE : (s + 1) * TILE, :].astype(F32)
                total = total + jnp.where(named[oi][s] == r, came, 0.0)
        wide, inverse = normalise(x_ref[0, rows, :])
        normed = wide * inverse
        mean = jnp.mean(total * normed, -1, keepdims=True)
        result = c_ref[0, rows, :].astype(F32) + inverse * (total - normed * mean)
        gf_ref[0, rows, :] = result.astype(BF16)
    advance(last, 5)
    advance(last, 6)
    out_copy(last).start()
    for oi in range(len(OFFSETS)):
        halo_copy(oi).wait_send()
        back_copy(oi).wait_send()

    def settle(h, carry):
        for phase in range(7):
            for copy in copies(h, phase):
                copy.wait_send()
        return carry

    lax.fori_loop(0, HEADS, settle, 0)
    for h in range(HEADS):
        out_copy(h).wait()


def on_device(dims, features, cotangent, weight_qkv, weight_out, key_tiles, tile_valid):
    patches, nz, ny, nx = dims
    group = nx
    half_rows = D // 2
    piece1 = half_rows // group
    piece2 = piece1 // group
    n_sem = 1 + 4 * (group - 1) + nz - 1 + 1
    n_off = len(OFFSETS)
    vmem = pl.BlockSpec(memory_space=pltpu.VMEM)
    smem = pl.BlockSpec(memory_space=pltpu.SMEM)
    grad_features, gathered = pl.pallas_call(
        functools.partial(kernel, dims),
        out_shape=(
            jax.ShapeDtypeStruct((1, ROWS, D), BF16),
            jax.ShapeDtypeStruct((HEADS, D, D), BF16),
        ),
        in_specs=[smem, smem, vmem, vmem, vmem, vmem],
        out_specs=(vmem, pl.BlockSpec(memory_space=pl.ANY)),
        scratch_shapes=[
            pltpu.VMEM((n_off, HALO, D), BF16),
            pltpu.VMEM((n_off, HALO, D), BF16),
            pltpu.VMEM((D, ALL), BF16),
            pltpu.VMEM((HEADS, ROWS, HW), BF16),
            pltpu.VMEM((HEADS, ALL, HW), BF16),
            pltpu.VMEM((HEADS, ALL, HW), BF16),
            pltpu.VMEM((HEADS, ROWS, HW), BF16),
            pltpu.VMEM((HEADS, HW, ROWS), BF16),
            pltpu.VMEM((HEADS, HW, ROWS), BF16),
            pltpu.VMEM((LOCAL, 8, 2 * ROWS), F32),
            pltpu.VMEM((ROWS, ALL), BF16),
            pltpu.VMEM((ROWS, ALL), BF16),
            pltpu.VMEM((HEADS, ROWS, HW), BF16),
            pltpu.VMEM((HEADS, ROWS, HW), BF16),
            pltpu.VMEM((2 * D, ALL), BF16),
            pltpu.VMEM((n_off, HALO, D), BF16),
            pltpu.VMEM((n_off, HALO, D), BF16),
            pltpu.VMEM((HEADS, D, D), BF16),
            pltpu.VMEM((HEADS, half_rows, D), BF16),
            pltpu.VMEM((HEADS, half_rows, D), BF16),
            pltpu.VMEM((HEADS, group - 1, piece1, D), BF16),
            pltpu.VMEM((HEADS, piece1, D), BF16),
            pltpu.VMEM((HEADS, group - 1, piece2, D), BF16),
            pltpu.VMEM((HEADS, nz, piece2, D), BF16),
            pltpu.VMEM((HEADS, D, D), BF16),
            pltpu.SemaphoreType.DMA((n_off,)),
            pltpu.SemaphoreType.DMA((n_off,)),
            pltpu.SemaphoreType.DMA((n_off,)),
            pltpu.SemaphoreType.DMA((n_off,)),
            pltpu.SemaphoreType.DMA((HEADS, n_sem)),
            pltpu.SemaphoreType.DMA((HEADS, n_sem)),
            pltpu.SemaphoreType.DMA((HEADS,)),
        ],
        compiler_params=pltpu.CompilerParams(
            collective_id=0, has_side_effects=True, vmem_limit_bytes=48 * 1024 * 1024
        ),
        cost_estimate=pl.CostEstimate(
            flops=8 * 10**9, bytes_accessed=8 * 2**20, transcendentals=2 * 2**20
        ),
        name="layer",
    )(key_tiles, tile_valid, features, cotangent, weight_qkv, weight_out)
    factor = float(patches * nx * ROWS) ** (-0.5)
    grad_qkv = gathered[:, :, : 3 * HW].reshape(HEADS, D, 3, HW).transpose(1, 2, 0, 3)
    grad_out = gathered[:, :, 3 * HW :].reshape(HEADS, D // HW, HW, HW).transpose(0, 2, 1, 3)
    return (
        grad_features,
        grad_qkv.reshape(D, 3 * D).astype(F32) * factor,
        grad_out.reshape(D, D).astype(F32) * factor,
    )


def solution(mesh):
    patches = mesh.shape["patch"]
    dims = (patches, patches // (2 * CHIPS_Y), CHIPS_Y, mesh.shape["sample"])
    placed = (P("sample", "patch", None), P("sample", "patch", None), P(), P(), P(), P())
    return jax.shard_map(
        functools.partial(on_device, dims),
        mesh=mesh,
        in_specs=placed,
        out_specs=(P("sample", "patch", None), P(), P()),
        check_vma=False,
    )
```

```python
import functools

import jax
import jax.numpy as jnp
from jax import lax
from jax.experimental import pallas as pl
from jax.experimental.pallas import tpu as pltpu
from jax.sharding import PartitionSpec as P

HEADS = 4
TILE = 128
LOCAL = 4
REACH = 2
OFFSETS = [-2, -1, 1, 2]
CHIPS_Y = 4
EPS = 1e-06
MESH = pl.DeviceIdType.MESH
F32 = jnp.float32
BF16 = jnp.bfloat16
LOG2E = 1.4426950408889634
BETWEEN = []
AFTER = [0, 3, (0, 0), 1, 2, (0, 1), "own", (0, 2), (0, 3), "finish", (0, 4), (0, 5), (0, 6), (0, 7)]


ROWS = LOCAL * TILE
HALO = 2 * TILE
ALL = ROWS + len(OFFSETS) * HALO
D = 512
HW = D // HEADS
PER_CHUNK = 4
CHUNKS = HEADS // PER_CHUNK
CHUNK_ROWS = PER_CHUNK * D


def nn(a, b):
    return lax.dot_general(a, b, (((1,), (0,)), ((), ())), preferred_element_type=F32)


def nt(a, b):
    return lax.dot_general(a, b, (((1,), (1,)), ((), ())), preferred_element_type=F32)


def tt(a, b):
    return lax.dot_general(a, b, (((0,), (1,)), ((), ())), preferred_element_type=F32)


def tn(a, b):
    return lax.dot_general(a, b, (((0,), (0,)), ((), ())), preferred_element_type=F32)


def normalise(rows):
    wide = rows.astype(F32)
    inverse = lax.rsqrt(jnp.mean(wide * wide, -1, keepdims=True) + EPS)
    return wide, inverse


def kernel(
    dims,
    kt,
    tv,
    x_hbm,
    c_hbm,
    w_hbm,
    wo_hbm,
    gf_hbm,
    out_ref,
    gf_ref,
    x_ref,
    c_ref,
    w_ref,
    wo_ref,
    stage,
    halo,
    normed_t,
    q,
    k,
    v,
    ga,
    q_t,
    ga_t,
    bias,
    prob,
    dscore,
    attended,
    dquery,
    dkv_t,
    back_out,
    back_in,
    local,
    got0,
    sum0,
    got1,
    sum1,
    got2,
    sum2,
    got3,
    res,
    halo_send,
    halo_recv,
    back_send,
    back_recv,
    red_send,
    red_recv,
    out_sem,
    in_sem,
):
    patches, nz, ny, nx = dims
    p = lax.axis_index("patch")
    sx = lax.axis_index("sample")
    core = lax.rem(p, 2)
    y = lax.rem(lax.div(p, 2), ny)
    z = lax.div(p, 2 * ny)

    def patch_at(zz, yy):
        return (zz * ny + yy) * 2 + core

    def first(j):
        return (
            patch_at(z, lax.rem(y + j * core, ny)),
            lax.rem(sx + j * (1 - core), nx),
        )

    def second(j):
        return (
            patch_at(z, lax.rem(y + j * (1 - core), ny)),
            lax.rem(sx + j * core, nx),
        )

    def along_z(j):
        return (patch_at(lax.rem(z + j, nz), y), sx)

    pair = (p + 1 - 2 * core, sx)
    m1 = sx * (1 - core) + y * core
    m2 = sx * core + y * (1 - core)
    group = nx

    loads = [
        pltpu.make_async_copy(src, dst, in_sem.at[i])
        for i, (src, dst) in enumerate(
            ((x_hbm, x_ref), (w_hbm, w_ref), (c_hbm, c_ref), (wo_hbm, wo_ref))
        )
    ]
    for load in loads:
        load.start()

    barrier = pltpu.get_barrier_semaphore()
    greeted = (
        [(lax.rem(p + o + patches, patches), sx) for o in OFFSETS]
        + [pair]
        + [first(j) for j in range(1, group)]
        + [second(j) for j in range(1, group)]
        + [along_z(j) for j in range(1, nz)]
    )
    for device in greeted:
        pl.semaphore_signal(barrier, inc=1, device_id=device, device_id_type=MESH)

    loads[0].wait()
    named = []
    for oi, o in enumerate(OFFSETS):
        row = lax.rem(p - o + patches, patches) * LOCAL
        one = kt[row, LOCAL + oi]
        two = one
        for r in range(1, LOCAL):
            entry = kt[row + r, LOCAL + oi]
            two = jnp.where(entry != one, entry, two)
        named.append((one - p * LOCAL, two - p * LOCAL))
        for s in range(2):
            tile = x_ref[0, 0:TILE, :]
            for r in range(1, LOCAL):
                tile = jnp.where(named[oi][s] == r, x_ref[0, r * TILE : (r + 1) * TILE, :], tile)
            stage[oi, s * TILE : (s + 1) * TILE, :] = tile

    pl.semaphore_wait(barrier, len(greeted))

    def halo_copy(oi):
        return pltpu.make_async_remote_copy(
            src_ref=stage.at[oi],
            dst_ref=halo.at[oi],
            send_sem=halo_send.at[oi],
            recv_sem=halo_recv.at[oi],
            device_id=(lax.rem(p - OFFSETS[oi] + patches, patches), sx),
            device_id_type=MESH,
        )

    def back_copy(oi):
        return pltpu.make_async_remote_copy(
            src_ref=back_out.at[oi],
            dst_ref=back_in.at[oi],
            send_sem=back_send.at[oi],
            recv_sem=back_recv.at[oi],
            device_id=(lax.rem(p + OFFSETS[oi] + patches, patches), sx),
            device_id_type=MESH,
        )

    for oi in (0, 3, 1, 2):
        halo_copy(oi).start()

    base = p * LOCAL
    pick = []
    for t in range(LOCAL):
        pick.append(
            [
                jnp.where(kt[base + t, LOCAL + n] != kt[base, LOCAL + n], 1, 0)
                for n in range(len(OFFSETS))
            ]
        )
        for r in range(LOCAL):
            flag = jnp.int32(0)
            for j in range(LOCAL):
                flag = flag + jnp.where(kt[base + t, j] == base + r, tv[base + t, j], 0)
            low = jnp.where(flag > 0, jnp.float32(0.0), jnp.float32(-1e30))
            bias[t, :, r * TILE : (r + 1) * TILE] = jnp.full((8, TILE), low, F32)
        for n in range(len(OFFSETS)):
            flag = tv[base + t, LOCAL + n]
            low = jnp.where(flag > 0, jnp.float32(0.0), jnp.float32(-1e30))
            bias[t, :, ROWS + n * TILE : ROWS + (n + 1) * TILE] = jnp.full((8, TILE), low, F32)

    loads[1].wait()
    wide, inverse = normalise(x_ref[0])
    low = (wide * inverse).astype(BF16)
    normed_t[:, 0:ROWS] = low.T
    for part, target in ((0, q), (1, k), (2, v)):
        for half in range(2):
            at = part * D + half * 2 * HW
            got = nn(low, w_ref[:, at : at + 2 * HW]).astype(BF16)
            for i in range(2):
                piece = got[:, i * HW : (i + 1) * HW]
                target[half * 2 + i, 0:ROWS, :] = piece
                if part == 0:
                    q_t[half * 2 + i] = piece.T
    loads[2].wait()
    loads[3].wait()
    for half in range(2):
        at = half * 2 * HW
        got = nt(c_ref[0], wo_ref[at : at + 2 * HW, :]).astype(BF16)
        for i in range(2):
            piece = got[:, i * HW : (i + 1) * HW]
            ga[half * 2 + i] = piece
            ga_t[half * 2 + i] = piece.T

    for oi in range(len(OFFSETS)):
        halo_copy(oi).wait_recv()
        wide, inverse = normalise(halo[oi])
        low = (wide * inverse).astype(BF16)
        at_row = ROWS + oi * HALO
        normed_t[:, at_row : at_row + HALO] = low.T
        for part, target in ((1, k), (2, v)):
            for half in range(2):
                at = part * D + half * 2 * HW
                got = nn(low, w_ref[:, at : at + 2 * HW]).astype(BF16)
                for i in range(2):
                    target[half * 2 + i, at_row : at_row + HALO, :] = got[:, i * HW : (i + 1) * HW]

    half_rows = CHUNK_ROWS // 2
    piece1 = half_rows // group
    piece2 = piece1 // group
    down, across = split_last(piece2, nz)
    piece3, width3 = piece2 // down, D // across
    base_row = core * half_rows
    at1 = base_row + m1 * piece1
    at2 = at1 + m2 * piece2
    n1 = group - 1
    counts = [1, n1, n1, nz - 1, nz - 1, n1, n1, 1]
    offsets = [sum(counts[:i]) for i in range(len(counts))]

    def rows_at(start, size):
        return pl.ds(pl.multiple_of(start, 16), size)

    def last_piece(index, start):
        return (
            rows_at(start + lax.div(index, across) * piece3, piece3),
            pl.ds(pl.multiple_of(lax.rem(index, across) * width3, 128), width3),
        )

    def copies(g, phase):
        if phase == 0:
            src = local.at[g, rows_at((1 - core) * half_rows, half_rows), :]
            moves = [(src, got0.at[g], pair)]
        elif phase == 1:
            moves = [
                (
                    sum0.at[g, rows_at(lax.rem(m1 + j, group) * piece1, piece1), :],
                    got1.at[g, j - 1],
                    first(j),
                )
                for j in range(1, group)
            ]
        elif phase == 2:
            moves = [
                (
                    sum1.at[g, rows_at(lax.rem(m2 + j, group) * piece2, piece2), :],
                    got2.at[g, j - 1],
                    second(j),
                )
                for j in range(1, group)
            ]
        elif phase == 3:
            moves = []
            for j in range(1, nz):
                at, columns = last_piece(lax.rem(z + j, nz), 0)
                moves.append((sum2.at[g, at, columns], got3.at[g, j - 1], along_z(j)))
        elif phase == 4:
            at, columns = last_piece(z, at2)
            mine = res.at[g, at, columns]
            moves = [(mine, mine, along_z(j)) for j in range(1, nz)]
        elif phase == 5:
            mine = res.at[g, rows_at(at2, piece2), :]
            moves = [(mine, mine, second(j)) for j in range(1, group)]
        elif phase == 6:
            mine = res.at[g, rows_at(at1, piece1), :]
            moves = [(mine, mine, first(j)) for j in range(1, group)]
        else:
            mine = res.at[g, rows_at(base_row, half_rows), :]
            moves = [(mine, mine, pair)]
        return [
            pltpu.make_async_remote_copy(
                src_ref=src,
                dst_ref=dst,
                send_sem=red_send.at[g, offsets[phase] + i],
                recv_sem=red_recv.at[g, offsets[phase] + i],
                device_id=device,
                device_id_type=MESH,
            )
            for i, (src, dst, device) in enumerate(moves)
        ]

    def start(g, phase):
        for copy in copies(g, phase):
            copy.start()

    def advance(g, phase):
        for copy in copies(g, phase):
            copy.wait_recv()
        if phase == 0:
            mine = local[g, rows_at(base_row, half_rows), :].astype(F32)
            sum0[g] = (mine + got0[g].astype(F32)).astype(BF16)
        if phase == 1:
            total = sum0[g, rows_at(m1 * piece1, piece1), :].astype(F32)
            for j in range(n1):
                total = total + got1[g, j].astype(F32)
            sum1[g] = total.astype(BF16)
        if phase == 2:
            total = sum1[g, rows_at(m2 * piece2, piece2), :].astype(F32)
            for j in range(n1):
                total = total + got2[g, j].astype(F32)
            sum2[g] = total.astype(BF16)
        if phase == 3:
            at, columns = last_piece(z, 0)
            total = sum2[g, at, columns].astype(F32)
            for j in range(nz - 1):
                total = total + got3[g, j].astype(F32)
            at, columns = last_piece(z, at2)
            res[g, at, columns] = total.astype(BF16)
        if phase < 7:
            start(g, phase + 1)

    scaling = HW ** (-0.5)

    def head(h, carry):
        for t in range(LOCAL):
            rows = slice(t * TILE, (t + 1) * TILE)

            def chosen(ref):
                parts = [ref[h, 0:ROWS, :]]
                for n in range(len(OFFSETS)):
                    at = ROWS + n * HALO
                    near = ref[h, at : at + TILE, :]
                    far = ref[h, at + TILE : at + HALO, :]
                    parts.append(jnp.where(pick[t][n] == 0, near, far))
                return jnp.concatenate(parts, 0)

            keys = chosen(k)
            values = chosen(v)
            scores = nt(q[h, rows, :], keys) + bias[t, 0:1, :]
            highest = jnp.max(scores, -1, keepdims=True)
            expanded = jnp.exp2((scores - highest) * (scaling * LOG2E))
            attention = expanded * (1.0 / jnp.sum(expanded, -1, keepdims=True))
            attention_low = attention.astype(BF16)
            dprob = nt(ga[h, rows, :], values)
            centre = jnp.sum(attention * dprob, -1, keepdims=True)
            ds = (attention * (dprob - centre) * scaling).astype(BF16)
            attended[h, rows, :] = nn(attention_low, values).astype(BF16)
            dquery[h, rows, :] = nn(ds, keys).astype(BF16)
            for full, piece in ((prob, attention_low), (dscore, ds)):
                full[rows, 0:ROWS] = piece[:, 0:ROWS]
                for n in range(len(OFFSETS)):
                    part = piece[:, ROWS + n * TILE : ROWS + (n + 1) * TILE]
                    for s in range(2):
                        at = ROWS + (2 * n + s) * TILE
                        keep = jnp.where(pick[t][n] == s, 1.0, 0.0).astype(BF16)
                        full[rows, at : at + TILE] = part * keep

            for when, g, phase in BETWEEN:
                if when % LOCAL == t:

                    @pl.when(h == when // LOCAL)
                    def _():
                        advance(g, phase)

        at = pl.multiple_of(h * HW, HW)
        dk = nn(q_t[h], dscore[...]).astype(BF16)
        dv = nn(ga_t[h], prob[...]).astype(BF16)
        dkv_t[pl.ds(at, HW), :] = dk
        dkv_t[pl.ds(pl.multiple_of(D + h * HW, HW), HW), :] = dv
        g = lax.div(h, PER_CHUNK)
        top = lax.rem(h, PER_CHUNK) * D
        rows = rows_at(top, D)
        local[g, rows, 0:HW] = nn(normed_t[:, 0:ROWS], dquery[h]).astype(BF16)
        local[g, rows, HW : 2 * HW] = nt(normed_t[...], dk).astype(BF16)
        local[g, rows, 2 * HW : 3 * HW] = nt(normed_t[...], dv).astype(BF16)
        outer = tn(attended[h], c_ref[0]).astype(BF16)
        for r in range(D // HW):
            rows = rows_at(top + r * HW, HW)
            local[g, rows, 3 * HW :] = outer[:, r * HW : (r + 1) * HW]

        @pl.when(lax.rem(h, PER_CHUNK) == PER_CHUNK - 1)
        def _():
            start(g, 0)

        return carry

    lax.fori_loop(0, HEADS, head, 0)

    def give_back(oi):
        at = ROWS + oi * HALO
        back_out[oi] = tt(dkv_t[:, at : at + HALO], w_ref[:, D:]).astype(BF16)
        back_copy(oi).start()

    last = CHUNKS - 1
    grad = []

    def own_grad():
        total = tt(dkv_t[:, 0:ROWS], w_ref[:, D:])
        for h in range(HEADS):
            total = total + nt(dquery[h], w_ref[:, h * HW : (h + 1) * HW])
        grad.append(total)

    def finish_features():
        for oi in range(len(OFFSETS)):
            back_copy(oi).wait_recv()
        for r in range(LOCAL):
            rows = slice(r * TILE, (r + 1) * TILE)
            total = grad[0][rows]
            for oi in range(len(OFFSETS)):
                for s in range(2):
                    came = back_in[oi, s * TILE : (s + 1) * TILE, :].astype(F32)
                    total = total + jnp.where(named[oi][s] == r, came, 0.0)
            wide, inverse = normalise(x_ref[0, rows, :])
            normed = wide * inverse
            mean = jnp.mean(total * normed, -1, keepdims=True)
            result = c_ref[0, rows, :].astype(F32) + inverse * (total - normed * mean)
            gf_ref[0, rows, :] = result.astype(BF16)
        features_copy.start()

    def out_copy(g):
        return pltpu.make_async_copy(res.at[g], out_ref.at[g], out_sem.at[g])

    features_copy = pltpu.make_async_copy(gf_ref, gf_hbm, in_sem.at[4])
    for step in AFTER:
        if step == "own":
            own_grad()
        elif step == "finish":
            finish_features()
        elif isinstance(step, int):
            give_back(step)
        else:
            g, phase = step
            advance(g, phase)
            if phase == 7:
                out_copy(g).start()
    for oi in range(len(OFFSETS)):
        halo_copy(oi).wait_send()
        back_copy(oi).wait_send()

    def settle(g, carry):
        for phase in range(8):
            for copy in copies(g, phase):
                copy.wait_send()
        return carry

    lax.fori_loop(0, CHUNKS, settle, 0)
    for g in range(CHUNKS):
        out_copy(g).wait()
    features_copy.wait()


def split_last(rows, count):
    down = min(count, rows // 16)
    return down, count // down


def finish(factor, chunks, features, qkv, out, grad_features):
    for h in range(HEADS):
        for part in range(3):
            piece = chunks[h, :, part * HW : (part + 1) * HW]
            at = part * D + h * HW
            qkv[:, at : at + HW] = piece.astype(F32) * factor
        out[h * HW : (h + 1) * HW, :] = chunks[h, :, 3 * HW :].astype(F32) * factor
    grad_features[...] = features[...]


def on_device(dims, features, cotangent, weight_qkv, weight_out, key_tiles, tile_valid):
    patches, nz, ny, nx = dims
    group = nx
    half_rows = CHUNK_ROWS // 2
    piece1 = half_rows // group
    piece2 = piece1 // group
    down, across = split_last(piece2, nz)
    n_sem = 2 + 4 * (group - 1) + 2 * (nz - 1)
    n_off = len(OFFSETS)
    smem = pl.BlockSpec(memory_space=pltpu.SMEM)
    grad_features, gathered = pl.pallas_call(
        functools.partial(kernel, dims),
        out_shape=(
            jax.ShapeDtypeStruct((1, ROWS, D), BF16),
            jax.ShapeDtypeStruct((CHUNKS, CHUNK_ROWS, D), BF16),
        ),
        in_specs=[smem, smem] + [pl.BlockSpec(memory_space=pltpu.HBM)] * 4,
        out_specs=(pl.BlockSpec(memory_space=pl.ANY), pl.BlockSpec(memory_space=pl.ANY)),
        scratch_shapes=[
            pltpu.VMEM((1, ROWS, D), BF16),
            pltpu.VMEM((1, ROWS, D), BF16),
            pltpu.VMEM((1, ROWS, D), BF16),
            pltpu.VMEM((D, 3 * D), BF16),
            pltpu.VMEM((D, D), BF16),
            pltpu.VMEM((n_off, HALO, D), BF16),
            pltpu.VMEM((n_off, HALO, D), BF16),
            pltpu.VMEM((D, ALL), BF16),
            pltpu.VMEM((HEADS, ROWS, HW), BF16),
            pltpu.VMEM((HEADS, ALL, HW), BF16),
            pltpu.VMEM((HEADS, ALL, HW), BF16),
            pltpu.VMEM((HEADS, ROWS, HW), BF16),
            pltpu.VMEM((HEADS, HW, ROWS), BF16),
            pltpu.VMEM((HEADS, HW, ROWS), BF16),
            pltpu.VMEM((LOCAL, 8, 2 * ROWS), F32),
            pltpu.VMEM((ROWS, ALL), BF16),
            pltpu.VMEM((ROWS, ALL), BF16),
            pltpu.VMEM((HEADS, ROWS, HW), BF16),
            pltpu.VMEM((HEADS, ROWS, HW), BF16),
            pltpu.VMEM((2 * D, ALL), BF16),
            pltpu.VMEM((n_off, HALO, D), BF16),
            pltpu.VMEM((n_off, HALO, D), BF16),
            pltpu.VMEM((CHUNKS, CHUNK_ROWS, D), BF16),
            pltpu.VMEM((CHUNKS, half_rows, D), BF16),
            pltpu.VMEM((CHUNKS, half_rows, D), BF16),
            pltpu.VMEM((CHUNKS, group - 1, piece1, D), BF16),
            pltpu.VMEM((CHUNKS, piece1, D), BF16),
            pltpu.VMEM((CHUNKS, group - 1, piece2, D), BF16),
            pltpu.VMEM((CHUNKS, piece2, D), BF16),
            pltpu.VMEM((CHUNKS, nz - 1, piece2 // down, D // across), BF16),
            pltpu.VMEM((CHUNKS, CHUNK_ROWS, D), BF16),
            pltpu.SemaphoreType.DMA((n_off,)),
            pltpu.SemaphoreType.DMA((n_off,)),
            pltpu.SemaphoreType.DMA((n_off,)),
            pltpu.SemaphoreType.DMA((n_off,)),
            pltpu.SemaphoreType.DMA((CHUNKS, n_sem)),
            pltpu.SemaphoreType.DMA((CHUNKS, n_sem)),
            pltpu.SemaphoreType.DMA((CHUNKS,)),
            pltpu.SemaphoreType.DMA((5,)),
        ],
        compiler_params=pltpu.CompilerParams(
            collective_id=0, has_side_effects=True, vmem_limit_bytes=60 * 1024 * 1024
        ),
        cost_estimate=pl.CostEstimate(
            flops=8 * 10**9, bytes_accessed=8 * 2**20, transcendentals=2 * 2**20
        ),
        name="layer",
    )(key_tiles, tile_valid, features, cotangent, weight_qkv, weight_out)
    factor = float(patches * nx * ROWS) ** (-0.5)
    chunks = gathered.reshape(HEADS, D, D)
    grad_qkv, grad_out, grad_features = pl.pallas_call(
        functools.partial(finish, factor),
        grid=(D // HW,),
        out_shape=(
            jax.ShapeDtypeStruct((D, 3 * D), F32),
            jax.ShapeDtypeStruct((D, D), F32),
            jax.ShapeDtypeStruct((1, ROWS, D), BF16),
        ),
        in_specs=[
            pl.BlockSpec((HEADS, HW, D), lambda r: (0, r, 0)),
            pl.BlockSpec((1, HW, D), lambda r: (0, r, 0)),
        ],
        out_specs=(
            pl.BlockSpec((HW, 3 * D), lambda r: (r, 0)),
            pl.BlockSpec((D, HW), lambda r: (0, r)),
            pl.BlockSpec((1, HW, D), lambda r: (0, r, 0)),
        ),
        name="finish",
    )(chunks, grad_features)
    return grad_features, grad_qkv, grad_out


def solution(mesh):
    patches = mesh.shape["patch"]
    dims = (patches, patches // (2 * CHIPS_Y), CHIPS_Y, mesh.shape["sample"])
    placed = (P("sample", "patch", None), P("sample", "patch", None), P(), P(), P(), P())
    return jax.shard_map(
        functools.partial(on_device, dims),
        mesh=mesh,
        in_specs=placed,
        out_specs=(P("sample", "patch", None), P(), P()),
        check_vma=False,
    )
```

```python
import functools

import jax
import jax.numpy as jnp
from jax import lax
from jax.experimental import pallas as pl
from jax.experimental.pallas import tpu as pltpu
from jax.sharding import PartitionSpec as P

HEADS = 4
TILE = 128
LOCAL = 4
REACH = 2
OFFSETS = [-2, -1, 1, 2]
CHIPS_Y = 4
EPS = 1e-06
MESH = pl.DeviceIdType.MESH
F32 = jnp.float32
BF16 = jnp.bfloat16
LOG2E = 1.4426950408889634
ROWS = LOCAL * TILE
HALO = 2 * TILE
ALL = ROWS + len(OFFSETS) * HALO
D = 512
HW = D // HEADS
HALF = D // 2


def nn(a, b):
    return lax.dot_general(a, b, (((1,), (0,)), ((), ())), preferred_element_type=F32)


def nt(a, b):
    return lax.dot_general(a, b, (((1,), (1,)), ((), ())), preferred_element_type=F32)


def tt(a, b):
    return lax.dot_general(a, b, (((0,), (1,)), ((), ())), preferred_element_type=F32)


def tn(a, b):
    return lax.dot_general(a, b, (((0,), (0,)), ((), ())), preferred_element_type=F32)


def normalise(rows):
    wide = rows.astype(F32)
    inverse = lax.rsqrt(jnp.mean(wide * wide, -1, keepdims=True) + EPS)
    return wide, inverse


def kernel(
    dims,
    kt_hbm,
    tv_hbm,
    x_hbm,
    c_hbm,
    w_hbm,
    wo_hbm,
    gf_hbm,
    out_ref,
    kt,
    tv,
    gf_ref,
    x_ref,
    c_ref,
    w_ref,
    wo_ref,
    stage,
    halo,
    normed_t,
    q,
    k,
    v,
    ga,
    q_t,
    ga_t,
    bias,
    own_scores,
    own_dprob,
    prob,
    dscore,
    attended,
    dquery,
    dkv_t,
    back_out,
    back_in,
    local,
    got0,
    sum0,
    got1,
    sum1,
    got2,
    sum2,
    got3,
    res,
    halo_send,
    halo_recv,
    back_send,
    back_recv,
    red_send,
    red_recv,
    out_sem,
    in_sem,
):
    patches, nz, ny, nx = dims
    p = lax.axis_index("patch")
    sx = lax.axis_index("sample")
    core = lax.rem(p, 2)
    y = lax.rem(lax.div(p, 2), ny)
    z = lax.div(p, 2 * ny)

    def patch_at(zz, yy):
        return (zz * ny + yy) * 2 + core

    def first(j):
        return (
            patch_at(z, lax.rem(y + j * core, ny)),
            lax.rem(sx + j * (1 - core), nx),
        )

    def second(j):
        return (
            patch_at(z, lax.rem(y + j * (1 - core), ny)),
            lax.rem(sx + j * core, nx),
        )

    def along_z(j):
        return (patch_at(lax.rem(z + j, nz), y), sx)

    pair = (p + 1 - 2 * core, sx)
    m1 = sx * (1 - core) + y * core
    m2 = sx * core + y * (1 - core)
    group = nx

    loads = [
        pltpu.make_async_copy(src, dst, in_sem.at[i])
        for i, (src, dst) in enumerate(
            (
                (x_hbm, x_ref),
                (w_hbm, w_ref),
                (c_hbm, c_ref),
                (wo_hbm, wo_ref),
                (kt_hbm, kt),
                (tv_hbm, tv),
            )
        )
    ]
    for i in (4, 0, 5, 1, 2, 3):
        loads[i].start()

    barrier = pltpu.get_barrier_semaphore()
    greeted = (
        [(lax.rem(p + o + patches, patches), sx) for o in OFFSETS]
        + [pair]
        + [first(j) for j in range(1, group)]
        + [second(j) for j in range(1, group)]
        + [along_z(j) for j in range(1, nz)]
    )
    for device in greeted:
        pl.semaphore_signal(barrier, inc=1, device_id=device, device_id_type=MESH)

    loads[0].wait()
    loads[4].wait()
    named = []
    for oi, o in enumerate(OFFSETS):
        row = lax.rem(p - o + patches, patches) * LOCAL
        one = kt[row, LOCAL + oi]
        two = one
        for r in range(1, LOCAL):
            entry = kt[row + r, LOCAL + oi]
            two = jnp.where(entry != one, entry, two)
        named.append((one - p * LOCAL, two - p * LOCAL))
        for s in range(2):
            tile = x_ref[0, 0:TILE, :]
            for r in range(1, LOCAL):
                tile = jnp.where(named[oi][s] == r, x_ref[0, r * TILE : (r + 1) * TILE, :], tile)
            stage[oi, s * TILE : (s + 1) * TILE, :] = tile

    pl.semaphore_wait(barrier, len(greeted))

    def halo_copy(oi, o=None):
        o = OFFSETS[oi] if o is None else o
        return pltpu.make_async_remote_copy(
            src_ref=stage.at[oi],
            dst_ref=halo.at[oi],
            send_sem=halo_send.at[oi],
            recv_sem=halo_recv.at[oi],
            device_id=(lax.rem(p - o + patches, patches), sx),
            device_id_type=MESH,
        )

    def back_copy(oi):
        return pltpu.make_async_remote_copy(
            src_ref=back_out.at[oi],
            dst_ref=back_in.at[oi],
            send_sem=back_send.at[oi],
            recv_sem=back_recv.at[oi],
            device_id=(lax.rem(p + OFFSETS[oi] + patches, patches), sx),
            device_id_type=MESH,
        )

    for oi in (0, 3, 1, 2):
        halo_copy(oi).start()

    loads[5].wait()
    base = p * LOCAL
    pick = []
    for t in range(LOCAL):
        pick.append(
            [
                jnp.where(kt[base + t, LOCAL + n] != kt[base, LOCAL + n], 1, 0)
                for n in range(len(OFFSETS))
            ]
        )
        for r in range(LOCAL):
            flag = jnp.int32(0)
            for j in range(LOCAL):
                flag = flag + jnp.where(kt[base + t, j] == base + r, tv[base + t, j], 0)
            low = jnp.where(flag > 0, jnp.float32(0.0), jnp.float32(-1e30))
            bias[t, :, r * TILE : (r + 1) * TILE] = jnp.full((8, TILE), low, F32)
        for n in range(len(OFFSETS)):
            flag = tv[base + t, LOCAL + n]
            low = jnp.where(flag > 0, jnp.float32(0.0), jnp.float32(-1e30))
            bias[t, :, ROWS + n * TILE : ROWS + (n + 1) * TILE] = jnp.full((8, TILE), low, F32)

    loads[1].wait()
    wide, inverse = normalise(x_ref[0])
    low = (wide * inverse).astype(BF16)
    normed_t[:, 0:ROWS] = low.T
    for part, target in ((0, q), (1, k), (2, v)):
        for half in range(2):
            at = part * D + half * 2 * HW
            got = nn(low, w_ref[:, at : at + 2 * HW]).astype(BF16)
            for i in range(2):
                piece = got[:, i * HW : (i + 1) * HW]
                target[half * 2 + i, 0:ROWS, :] = piece
                if part == 0:
                    q_t[half * 2 + i] = piece.T
    loads[2].wait()
    loads[3].wait()
    for half in range(2):
        at = half * 2 * HW
        got = nt(c_ref[0], wo_ref[at : at + 2 * HW, :]).astype(BF16)
        for i in range(2):
            piece = got[:, i * HW : (i + 1) * HW]
            ga[half * 2 + i] = piece
            ga_t[half * 2 + i] = piece.T

    for h in range(HEADS):
        own_scores[h] = nt(q[h], k[h, 0:ROWS, :])
        own_dprob[h] = nt(ga[h], v[h, 0:ROWS, :])

    for oi, o in ((2 - core, 1 - 2 * core), (1 + core, 2 * core - 1), (0, -2), (3, 2)):
        halo_copy(oi, o).wait_recv()
        wide, inverse = normalise(halo[oi])
        low = (wide * inverse).astype(BF16)
        at_row = pl.ds(pl.multiple_of(ROWS + oi * HALO, HALO), HALO)
        normed_t[:, at_row] = low.T
        for part, target in ((1, k), (2, v)):
            for half in range(2):
                at = part * D + half * 2 * HW
                got = nn(low, w_ref[:, at : at + 2 * HW]).astype(BF16)
                for i in range(2):
                    target[half * 2 + i, at_row, :] = got[:, i * HW : (i + 1) * HW]

    n1 = group - 1
    piece1 = HALF // group
    per_owner = HEADS // group
    piece2 = per_owner * piece1
    down, across = split_last(piece2, nz)
    piece3, width3 = piece2 // down, D // across
    half_at = core * HALF
    at1 = half_at + m1 * piece1
    counts = reduction_counts(group, nz)
    firsts = [sum(counts[:i]) for i in range(len(counts))]

    def rows_at(start, size):
        return pl.ds(pl.multiple_of(start, 16), size)

    def owned(owner):
        return pl.ds(owner * per_owner, per_owner)

    def last_piece(index):
        return (
            rows_at(lax.div(index, across) * piece3, piece3),
            pl.ds(pl.multiple_of(lax.rem(index, across) * width3, 128), width3),
        )

    def last_place(index):
        row = lax.div(index, across) * piece3
        head_at = m2 * per_owner + lax.div(row, piece1)
        rows = rows_at(at1 + lax.rem(row, piece1), piece3)
        return head_at, rows, last_piece(index)[1]

    def move(phase, i, src, dst, device):
        return pltpu.make_async_remote_copy(
            src_ref=src,
            dst_ref=dst,
            send_sem=red_send.at[firsts[phase] + i],
            recv_sem=red_recv.at[firsts[phase] + i],
            device_id=device,
            device_id_type=MESH,
        )

    def to_pair(h):
        src = local.at[h, rows_at((1 - core) * HALF, HALF), :]
        return [move(0, h, src, got0.at[h], pair)]

    def scatter_first(h):
        return [
            move(
                1,
                h * n1 + j - 1,
                sum0.at[h, rows_at(lax.rem(m1 + j, group) * piece1, piece1), :],
                got1.at[h, j - 1],
                first(j),
            )
            for j in range(1, group)
        ]

    def scatter_second():
        return [
            move(
                2,
                j - 1,
                sum1.at[rows_at(lax.rem(m2 + j, group) * piece2, piece2), :],
                got2.at[j - 1],
                second(j),
            )
            for j in range(1, group)
        ]

    def scatter_z():
        moves = []
        for j in range(1, nz):
            rows, columns = last_piece(lax.rem(z + j, nz))
            moves.append(move(3, j - 1, sum2.at[rows, columns], got3.at[j - 1], along_z(j)))
        return moves

    def gather_z():
        mine = res.at[last_place(z)]
        return [move(4, j - 1, mine, mine, along_z(j)) for j in range(1, nz)]

    def gather_second():
        mine = res.at[owned(m2), rows_at(at1, piece1), :]
        return [move(5, j - 1, mine, mine, second(j)) for j in range(1, group)]

    def gather_first(i):
        mine = res.at[owned(lax.rem(m2 - i + group, group)), rows_at(at1, piece1), :]
        return [move(6, i * n1 + j - 1, mine, mine, first(j)) for j in range(1, group)]

    def gather_pair(i):
        mine = res.at[owned(lax.rem(m2 - i + group, group)), rows_at(half_at, HALF), :]
        return [move(7, i, mine, mine, pair)]

    def start(copies):
        for copy in copies:
            copy.start()

    def arrive(copies):
        for copy in copies:
            copy.wait_recv()

    def add_pair(h):
        arrive(to_pair(h))
        mine = local[h, rows_at(half_at, HALF), :].astype(F32)
        sum0[h] = (mine + got0[h].astype(F32)).astype(BF16)
        start(scatter_first(h))

    def add_first(h):
        arrive(scatter_first(h))
        total = sum0[h, rows_at(m1 * piece1, piece1), :].astype(F32)
        for j in range(n1):
            total = total + got1[h, j].astype(F32)
        sum1[h * piece1 : (h + 1) * piece1, :] = total.astype(BF16)

    def add_second():
        arrive(scatter_second())
        total = sum1[rows_at(m2 * piece2, piece2), :].astype(F32)
        for j in range(n1):
            total = total + got2[j].astype(F32)
        sum2[...] = total.astype(BF16)
        start(scatter_z())

    def add_z():
        arrive(scatter_z())
        total = sum2[last_piece(z)].astype(F32)
        for j in range(nz - 1):
            total = total + got3[j].astype(F32)
        res[last_place(z)] = total.astype(BF16)
        start(gather_z())

    scaling = HW ** (-0.5)

    def head(h, carry):
        for t in range(LOCAL):
            rows = slice(t * TILE, (t + 1) * TILE)

            def chosen(ref):
                parts = [ref[h, 0:ROWS, :]]
                for n in range(len(OFFSETS)):
                    at = ROWS + n * HALO
                    near = ref[h, at : at + TILE, :]
                    far = ref[h, at + TILE : at + HALO, :]
                    parts.append(jnp.where(pick[t][n] == 0, near, far))
                return jnp.concatenate(parts, 0)

            keys = chosen(k)
            values = chosen(v)
            scores = jnp.concatenate(
                [own_scores[h, rows, :], nt(q[h, rows, :], keys[ROWS:])], 1
            )
            scores = scores + bias[t, 0:1, :]
            highest = jnp.max(scores, -1, keepdims=True)
            expanded = jnp.exp2((scores - highest) * (scaling * LOG2E))
            attention = expanded * (1.0 / jnp.sum(expanded, -1, keepdims=True))
            attention_low = attention.astype(BF16)
            dprob = jnp.concatenate(
                [own_dprob[h, rows, :], nt(ga[h, rows, :], values[ROWS:])], 1
            )
            centre = jnp.sum(attention * dprob, -1, keepdims=True)
            ds = (attention * (dprob - centre) * scaling).astype(BF16)
            attended[h, rows, :] = nn(attention_low, values).astype(BF16)
            dquery[h, rows, :] = nn(ds, keys).astype(BF16)
            for full, piece in ((prob, attention_low), (dscore, ds)):
                full[rows, 0:ROWS] = piece[:, 0:ROWS]
                for n in range(len(OFFSETS)):
                    part = piece[:, ROWS + n * TILE : ROWS + (n + 1) * TILE]
                    for s in range(2):
                        at = ROWS + (2 * n + s) * TILE
                        keep = jnp.where(pick[t][n] == s, 1.0, 0.0).astype(BF16)
                        full[rows, at : at + TILE] = part * keep

            if t == 2:

                @pl.when(h >= 1)
                def _():
                    add_pair(h - 1)

        at = pl.multiple_of(h * HW, HW)
        dk = nn(q_t[h], dscore[...]).astype(BF16)
        dv = nn(ga_t[h], prob[...]).astype(BF16)
        dkv_t[pl.ds(at, HW), :] = dk
        dkv_t[pl.ds(pl.multiple_of(D + h * HW, HW), HW), :] = dv
        local[h, :, 0:HW] = nn(normed_t[:, 0:ROWS], dquery[h]).astype(BF16)
        local[h, :, HW : 2 * HW] = nt(normed_t[...], dk).astype(BF16)
        local[h, :, 2 * HW : 3 * HW] = nt(normed_t[...], dv).astype(BF16)
        outer = tn(attended[h], c_ref[0]).astype(BF16)
        for r in range(D // HW):
            local[h, r * HW : (r + 1) * HW, 3 * HW :] = outer[:, r * HW : (r + 1) * HW]
        start(to_pair(h))
        return carry

    lax.fori_loop(0, HEADS, head, 0)

    def give_back(oi):
        at = ROWS + oi * HALO
        back_out[oi] = tt(dkv_t[:, at : at + HALO], w_ref[:, D:]).astype(BF16)
        back_copy(oi).start()

    def own_grad():
        total = tt(dkv_t[:, 0:ROWS], w_ref[:, D:])
        for h in range(HEADS):
            total = total + nt(dquery[h], w_ref[:, h * HW : (h + 1) * HW])
        return total

    def finish_features(grad):
        for oi in range(len(OFFSETS)):
            back_copy(oi).wait_recv()
        for r in range(LOCAL):
            rows = slice(r * TILE, (r + 1) * TILE)
            total = grad[rows]
            for oi in range(len(OFFSETS)):
                for s in range(2):
                    came = back_in[oi, s * TILE : (s + 1) * TILE, :].astype(F32)
                    total = total + jnp.where(named[oi][s] == r, came, 0.0)
            wide, inverse = normalise(x_ref[0, rows, :])
            normed = wide * inverse
            mean = jnp.mean(total * normed, -1, keepdims=True)
            result = c_ref[0, rows, :].astype(F32) + inverse * (total - normed * mean)
            gf_ref[0, rows, :] = result.astype(BF16)
        features_copy.start()

    out_copy = pltpu.make_async_copy(res, out_ref, out_sem)
    features_copy = pltpu.make_async_copy(gf_ref, gf_hbm, in_sem.at[6])
    give_back(0)
    give_back(3)
    add_pair(HEADS - 1)
    give_back(1)
    give_back(2)
    for h in range(HEADS):
        add_first(h)
    start(scatter_second())
    grad = own_grad()
    add_second()
    add_z()
    finish_features(grad)
    arrive(gather_z())
    start(gather_second())
    start(gather_first(0))
    for j in range(1, group):
        arrive(gather_second()[j - 1 : j])
        start(gather_first(j))
    for i in range(group):
        arrive(gather_first(i))
        start(gather_pair(i))
    for i in range(group):
        arrive(gather_pair(i))
    out_copy.start()
    for oi in range(len(OFFSETS)):
        halo_copy(oi).wait_send()
        back_copy(oi).wait_send()

    def settle(h, carry):
        for copy in to_pair(h) + scatter_first(h):
            copy.wait_send()
        return carry

    lax.fori_loop(0, HEADS, settle, 0)
    for copy in scatter_second() + scatter_z() + gather_z() + gather_second():
        copy.wait_send()
    for i in range(group):
        for copy in gather_first(i) + gather_pair(i):
            copy.wait_send()
    out_copy.wait()
    features_copy.wait()


def reduction_counts(group, nz):
    n1 = group - 1
    return [HEADS, HEADS * n1, n1, nz - 1, nz - 1, n1, group * n1, group]


def split_last(rows, count):
    down = min(count, rows // 16)
    return down, count // down


def finish(factor, chunks, features, qkv, out, grad_features):
    for h in range(HEADS):
        for part in range(3):
            piece = chunks[h, :, part * HW : (part + 1) * HW]
            at = part * D + h * HW
            qkv[:, at : at + HW] = piece.astype(F32) * factor
        out[h * HW : (h + 1) * HW, :] = chunks[h, :, 3 * HW :].astype(F32) * factor
    grad_features[...] = features[...]


def on_device(dims, features, cotangent, weight_qkv, weight_out, key_tiles, tile_valid):
    patches, nz, ny, nx = dims
    group = nx
    piece1 = HALF // group
    piece2 = HEADS // group * piece1
    down, across = split_last(piece2, nz)
    n_sem = sum(reduction_counts(group, nz))
    n_off = len(OFFSETS)
    grad_features, gathered = pl.pallas_call(
        functools.partial(kernel, dims),
        out_shape=(
            jax.ShapeDtypeStruct((1, ROWS, D), BF16),
            jax.ShapeDtypeStruct((HEADS, D, D), BF16),
        ),
        in_specs=[pl.BlockSpec(memory_space=pltpu.HBM)] * 6,
        out_specs=(pl.BlockSpec(memory_space=pl.ANY), pl.BlockSpec(memory_space=pl.ANY)),
        scratch_shapes=[
            pltpu.SMEM(key_tiles.shape, jnp.int32),
            pltpu.SMEM(tile_valid.shape, jnp.int32),
            pltpu.VMEM((1, ROWS, D), BF16),
            pltpu.VMEM((1, ROWS, D), BF16),
            pltpu.VMEM((1, ROWS, D), BF16),
            pltpu.VMEM((D, 3 * D), BF16),
            pltpu.VMEM((D, D), BF16),
            pltpu.VMEM((n_off, HALO, D), BF16),
            pltpu.VMEM((n_off, HALO, D), BF16),
            pltpu.VMEM((D, ALL), BF16),
            pltpu.VMEM((HEADS, ROWS, HW), BF16),
            pltpu.VMEM((HEADS, ALL, HW), BF16),
            pltpu.VMEM((HEADS, ALL, HW), BF16),
            pltpu.VMEM((HEADS, ROWS, HW), BF16),
            pltpu.VMEM((HEADS, HW, ROWS), BF16),
            pltpu.VMEM((HEADS, HW, ROWS), BF16),
            pltpu.VMEM((LOCAL, 8, 2 * ROWS), F32),
            pltpu.VMEM((HEADS, ROWS, ROWS), F32),
            pltpu.VMEM((HEADS, ROWS, ROWS), F32),
            pltpu.VMEM((ROWS, ALL), BF16),
            pltpu.VMEM((ROWS, ALL), BF16),
            pltpu.VMEM((HEADS, ROWS, HW), BF16),
            pltpu.VMEM((HEADS, ROWS, HW), BF16),
            pltpu.VMEM((2 * D, ALL), BF16),
            pltpu.VMEM((n_off, HALO, D), BF16),
            pltpu.VMEM((n_off, HALO, D), BF16),
            pltpu.VMEM((HEADS, D, D), BF16),
            pltpu.VMEM((HEADS, HALF, D), BF16),
            pltpu.VMEM((HEADS, HALF, D), BF16),
            pltpu.VMEM((HEADS, group - 1, piece1, D), BF16),
            pltpu.VMEM((HEADS * piece1, D), BF16),
            pltpu.VMEM((group - 1, piece2, D), BF16),
            pltpu.VMEM((piece2, D), BF16),
            pltpu.VMEM((nz - 1, piece2 // down, D // across), BF16),
            pltpu.VMEM((HEADS, D, D), BF16),
            pltpu.SemaphoreType.DMA((n_off,)),
            pltpu.SemaphoreType.DMA((n_off,)),
            pltpu.SemaphoreType.DMA((n_off,)),
            pltpu.SemaphoreType.DMA((n_off,)),
            pltpu.SemaphoreType.DMA((n_sem,)),
            pltpu.SemaphoreType.DMA((n_sem,)),
            pltpu.SemaphoreType.DMA,
            pltpu.SemaphoreType.DMA((7,)),
        ],
        compiler_params=pltpu.CompilerParams(
            collective_id=0, has_side_effects=True, vmem_limit_bytes=60 * 1024 * 1024
        ),
        cost_estimate=pl.CostEstimate(
            flops=8 * 10**9, bytes_accessed=8 * 2**20, transcendentals=2 * 2**20
        ),
        name="layer",
    )(key_tiles, tile_valid, features, cotangent, weight_qkv, weight_out)
    factor = float(patches * nx * ROWS) ** (-0.5)
    grad_qkv, grad_out, grad_features = pl.pallas_call(
        functools.partial(finish, factor),
        grid=(D // HW,),
        out_shape=(
            jax.ShapeDtypeStruct((D, 3 * D), F32),
            jax.ShapeDtypeStruct((D, D), F32),
            jax.ShapeDtypeStruct((1, ROWS, D), BF16),
        ),
        in_specs=[
            pl.BlockSpec((HEADS, HW, D), lambda r: (0, r, 0)),
            pl.BlockSpec((1, HW, D), lambda r: (0, r, 0)),
        ],
        out_specs=(
            pl.BlockSpec((HW, 3 * D), lambda r: (r, 0)),
            pl.BlockSpec((D, HW), lambda r: (0, r)),
            pl.BlockSpec((1, HW, D), lambda r: (0, r, 0)),
        ),
        name="finish",
    )(gathered, grad_features)
    return grad_features, grad_qkv, grad_out


def solution(mesh):
    patches = mesh.shape["patch"]
    dims = (patches, patches // (2 * CHIPS_Y), CHIPS_Y, mesh.shape["sample"])
    placed = (P("sample", "patch", None), P("sample", "patch", None), P(), P(), P(), P())
    return jax.shard_map(
        functools.partial(on_device, dims),
        mesh=mesh,
        in_specs=placed,
        out_specs=(P("sample", "patch", None), P(), P()),
        check_vma=False,
    )
```

```python
import functools

import jax
import jax.numpy as jnp
from jax import lax
from jax.experimental import pallas as pl
from jax.experimental.pallas import tpu as pltpu
from jax.sharding import PartitionSpec as P

HEADS = 4
TILE = 128
LOCAL = 4
REACH = 2
OFFSETS = [-2, -1, 1, 2]
CHIPS_Y = 4
EPS = 1e-06
MESH = pl.DeviceIdType.MESH
F32 = jnp.float32
BF16 = jnp.bfloat16
LOG2E = 1.4426950408889634
ROWS = LOCAL * TILE
HALO = 2 * TILE
ALL = ROWS + len(OFFSETS) * HALO
D = 512
HW = D // HEADS
HALF = D // 2


def nn(a, b):
    return lax.dot_general(a, b, (((1,), (0,)), ((), ())), preferred_element_type=F32)


def nt(a, b):
    return lax.dot_general(a, b, (((1,), (1,)), ((), ())), preferred_element_type=F32)


def tt(a, b):
    return lax.dot_general(a, b, (((0,), (1,)), ((), ())), preferred_element_type=F32)


def tn(a, b):
    return lax.dot_general(a, b, (((0,), (0,)), ((), ())), preferred_element_type=F32)


def normalise(rows):
    wide = rows.astype(F32)
    inverse = lax.rsqrt(jnp.mean(wide * wide, -1, keepdims=True) + EPS)
    return wide, inverse


def kernel(
    dims,
    kt_hbm,
    tv_hbm,
    x_hbm,
    c_hbm,
    w_hbm,
    wo_hbm,
    gf_hbm,
    out_ref,
    kt,
    tv,
    gf_ref,
    x_ref,
    c_ref,
    w_ref,
    wo_ref,
    stage,
    halo,
    normed_t,
    q,
    k,
    v,
    ga,
    q_t,
    ga_t,
    bias,
    own_scores,
    own_dprob,
    prob,
    dscore,
    attended,
    dquery,
    dkv_t,
    back_out,
    back_in,
    local,
    got0,
    sum0,
    got1,
    sum1,
    got2,
    sum2,
    got3,
    res,
    halo_send,
    halo_recv,
    back_send,
    back_recv,
    red_send,
    red_recv,
    out_sem,
    in_sem,
):
    patches, nz, ny, nx = dims
    p = lax.axis_index("patch")
    sx = lax.axis_index("sample")
    core = lax.rem(p, 2)
    y = lax.rem(lax.div(p, 2), ny)
    z = lax.div(p, 2 * ny)

    def patch_at(zz, yy):
        return (zz * ny + yy) * 2 + core

    def first(j):
        return (
            patch_at(z, lax.rem(y + j * core, ny)),
            lax.rem(sx + j * (1 - core), nx),
        )

    def second(j):
        return (
            patch_at(z, lax.rem(y + j * (1 - core), ny)),
            lax.rem(sx + j * core, nx),
        )

    def along_z(j):
        return (patch_at(lax.rem(z + j, nz), y), sx)

    pair = (p + 1 - 2 * core, sx)
    m1 = sx * (1 - core) + y * core
    m2 = sx * core + y * (1 - core)
    group = nx

    loads = [
        pltpu.make_async_copy(src, dst, in_sem.at[i])
        for i, (src, dst) in enumerate(
            (
                (x_hbm, x_ref),
                (w_hbm, w_ref),
                (c_hbm, c_ref),
                (wo_hbm, wo_ref),
                (kt_hbm, kt),
                (tv_hbm, tv),
            )
        )
    ]
    for i in (4, 0, 5, 1, 2, 3):
        loads[i].start()

    barrier = pltpu.get_barrier_semaphore()
    greeted = (
        [(lax.rem(p + o + patches, patches), sx) for o in OFFSETS]
        + [pair]
        + [first(j) for j in range(1, group)]
        + [second(j) for j in range(1, group)]
        + [along_z(j) for j in range(1, nz)]
    )
    for device in greeted:
        pl.semaphore_signal(barrier, inc=1, device_id=device, device_id_type=MESH)

    loads[0].wait()
    loads[4].wait()
    named = []
    for oi, o in enumerate(OFFSETS):
        row = lax.rem(p - o + patches, patches) * LOCAL
        one = kt[LOCAL + oi, row]
        two = one
        for r in range(1, LOCAL):
            entry = kt[LOCAL + oi, row + r]
            two = jnp.where(entry != one, entry, two)
        named.append((one - p * LOCAL, two - p * LOCAL))
        for s in range(2):
            tile = x_ref[0, 0:TILE, :]
            for r in range(1, LOCAL):
                tile = jnp.where(named[oi][s] == r, x_ref[0, r * TILE : (r + 1) * TILE, :], tile)
            stage[oi, s * TILE : (s + 1) * TILE, :] = tile

    pl.semaphore_wait(barrier, len(greeted))

    def halo_copy(oi, o=None):
        o = OFFSETS[oi] if o is None else o
        return pltpu.make_async_remote_copy(
            src_ref=stage.at[oi],
            dst_ref=halo.at[oi],
            send_sem=halo_send.at[oi],
            recv_sem=halo_recv.at[oi],
            device_id=(lax.rem(p - o + patches, patches), sx),
            device_id_type=MESH,
        )

    def back_copy(oi):
        return pltpu.make_async_remote_copy(
            src_ref=back_out.at[oi],
            dst_ref=back_in.at[oi],
            send_sem=back_send.at[oi],
            recv_sem=back_recv.at[oi],
            device_id=(lax.rem(p + OFFSETS[oi] + patches, patches), sx),
            device_id_type=MESH,
        )

    for oi in (0, 3, 1, 2):
        halo_copy(oi).start()

    loads[5].wait()
    base = p * LOCAL
    pick = []
    for t in range(LOCAL):
        pick.append(
            [
                jnp.where(kt[LOCAL + n, base + t] != kt[LOCAL + n, base], 1, 0)
                for n in range(len(OFFSETS))
            ]
        )
        for r in range(LOCAL):
            flag = jnp.int32(0)
            for j in range(LOCAL):
                flag = flag + jnp.where(kt[j, base + t] == base + r, tv[j, base + t], 0)
            low = jnp.where(flag > 0, jnp.float32(0.0), jnp.float32(-1e30))
            bias[t, :, r * TILE : (r + 1) * TILE] = jnp.full((8, TILE), low, F32)
        for n in range(len(OFFSETS)):
            flag = tv[LOCAL + n, base + t]
            low = jnp.where(flag > 0, jnp.float32(0.0), jnp.float32(-1e30))
            bias[t, :, ROWS + n * TILE : ROWS + (n + 1) * TILE] = jnp.full((8, TILE), low, F32)

    loads[1].wait()
    wide, inverse = normalise(x_ref[0])
    low = (wide * inverse).astype(BF16)
    normed_t[:, 0:ROWS] = low.T
    for part, target in ((0, q), (1, k), (2, v)):
        for half in range(2):
            at = part * D + half * 2 * HW
            got = nn(low, w_ref[:, at : at + 2 * HW]).astype(BF16)
            for i in range(2):
                piece = got[:, i * HW : (i + 1) * HW]
                target[half * 2 + i, 0:ROWS, :] = piece
                if part == 0:
                    q_t[half * 2 + i] = piece.T
    loads[2].wait()
    loads[3].wait()
    for half in range(2):
        at = half * 2 * HW
        got = nt(c_ref[0], wo_ref[at : at + 2 * HW, :]).astype(BF16)
        for i in range(2):
            piece = got[:, i * HW : (i + 1) * HW]
            ga[half * 2 + i] = piece
            ga_t[half * 2 + i] = piece.T

    for h in range(HEADS):
        own_scores[h] = nt(q[h], k[h, 0:ROWS, :])
        own_dprob[h] = nt(ga[h], v[h, 0:ROWS, :])

    for oi, o in ((2 - core, 1 - 2 * core), (1 + core, 2 * core - 1), (0, -2), (3, 2)):
        halo_copy(oi, o).wait_recv()
        wide, inverse = normalise(halo[oi])
        low = (wide * inverse).astype(BF16)
        at_row = pl.ds(pl.multiple_of(ROWS + oi * HALO, HALO), HALO)
        normed_t[:, at_row] = low.T
        for part, target in ((1, k), (2, v)):
            for half in range(2):
                at = part * D + half * 2 * HW
                got = nn(low, w_ref[:, at : at + 2 * HW]).astype(BF16)
                for i in range(2):
                    target[half * 2 + i, at_row, :] = got[:, i * HW : (i + 1) * HW]

    n1 = group - 1
    piece1 = HALF // group
    per_owner = HEADS // group
    piece2 = per_owner * piece1
    down, across = split_last(piece2, nz)
    piece3, width3 = piece2 // down, D // across
    half_at = core * HALF
    at1 = half_at + m1 * piece1
    counts = reduction_counts(group, nz)
    firsts = [sum(counts[:i]) for i in range(len(counts))]

    def rows_at(start, size):
        return pl.ds(pl.multiple_of(start, 16), size)

    def owned(owner):
        return pl.ds(owner * per_owner, per_owner)

    def last_piece(index):
        return (
            rows_at(lax.div(index, across) * piece3, piece3),
            pl.ds(pl.multiple_of(lax.rem(index, across) * width3, 128), width3),
        )

    def last_place(index):
        row = lax.div(index, across) * piece3
        head_at = m2 * per_owner + lax.div(row, piece1)
        rows = rows_at(at1 + lax.rem(row, piece1), piece3)
        return head_at, rows, last_piece(index)[1]

    def move(phase, i, src, dst, device):
        return pltpu.make_async_remote_copy(
            src_ref=src,
            dst_ref=dst,
            send_sem=red_send.at[firsts[phase] + i],
            recv_sem=red_recv.at[firsts[phase] + i],
            device_id=device,
            device_id_type=MESH,
        )

    def to_pair(h):
        src = local.at[h, rows_at((1 - core) * HALF, HALF), :]
        return [move(0, h, src, got0.at[h], pair)]

    def scatter_first(h):
        return [
            move(
                1,
                h * n1 + j - 1,
                sum0.at[h, rows_at(lax.rem(m1 + j, group) * piece1, piece1), :],
                got1.at[h, j - 1],
                first(j),
            )
            for j in range(1, group)
        ]

    def scatter_second():
        return [
            move(
                2,
                j - 1,
                sum1.at[rows_at(lax.rem(m2 + j, group) * piece2, piece2), :],
                got2.at[j - 1],
                second(j),
            )
            for j in range(1, group)
        ]

    def scatter_z():
        moves = []
        for j in range(1, nz):
            rows, columns = last_piece(lax.rem(z + j, nz))
            moves.append(move(3, j - 1, sum2.at[rows, columns], got3.at[j - 1], along_z(j)))
        return moves

    def gather_z():
        mine = res.at[last_place(z)]
        return [move(4, j - 1, mine, mine, along_z(j)) for j in range(1, nz)]

    def gather_second():
        mine = res.at[owned(m2), rows_at(at1, piece1), :]
        return [move(5, j - 1, mine, mine, second(j)) for j in range(1, group)]

    def gather_first(i):
        mine = res.at[owned(lax.rem(m2 - i + group, group)), rows_at(at1, piece1), :]
        return [move(6, i * n1 + j - 1, mine, mine, first(j)) for j in range(1, group)]

    def gather_pair(i):
        mine = res.at[owned(lax.rem(m2 - i + group, group)), rows_at(half_at, HALF), :]
        return [move(7, i, mine, mine, pair)]

    def start(copies):
        for copy in copies:
            copy.start()

    def arrive(copies):
        for copy in copies:
            copy.wait_recv()

    def add_pair(h):
        arrive(to_pair(h))
        mine = local[h, rows_at(half_at, HALF), :].astype(F32)
        sum0[h] = (mine + got0[h].astype(F32)).astype(BF16)
        start(scatter_first(h))

    def add_first(h):
        arrive(scatter_first(h))
        total = sum0[h, rows_at(m1 * piece1, piece1), :].astype(F32)
        for j in range(n1):
            total = total + got1[h, j].astype(F32)
        sum1[h * piece1 : (h + 1) * piece1, :] = total.astype(BF16)

    def add_second():
        arrive(scatter_second())
        total = sum1[rows_at(m2 * piece2, piece2), :].astype(F32)
        for j in range(n1):
            total = total + got2[j].astype(F32)
        sum2[...] = total.astype(BF16)
        start(scatter_z())

    def add_z():
        arrive(scatter_z())
        total = sum2[last_piece(z)].astype(F32)
        for j in range(nz - 1):
            total = total + got3[j].astype(F32)
        res[last_place(z)] = total.astype(BF16)
        start(gather_z())

    scaling = HW ** (-0.5)

    def head(h, carry):
        for t in range(LOCAL):
            rows = slice(t * TILE, (t + 1) * TILE)

            def chosen(ref):
                parts = [ref[h, 0:ROWS, :]]
                for n in range(len(OFFSETS)):
                    at = ROWS + n * HALO
                    near = ref[h, at : at + TILE, :]
                    far = ref[h, at + TILE : at + HALO, :]
                    parts.append(jnp.where(pick[t][n] == 0, near, far))
                return jnp.concatenate(parts, 0)

            keys = chosen(k)
            values = chosen(v)
            scores = jnp.concatenate(
                [own_scores[h, rows, :], nt(q[h, rows, :], keys[ROWS:])], 1
            )
            scores = scores + bias[t, 0:1, :]
            highest = jnp.max(scores, -1, keepdims=True)
            expanded = jnp.exp2((scores - highest) * (scaling * LOG2E))
            attention = expanded * (1.0 / jnp.sum(expanded, -1, keepdims=True))
            attention_low = attention.astype(BF16)
            dprob = jnp.concatenate(
                [own_dprob[h, rows, :], nt(ga[h, rows, :], values[ROWS:])], 1
            )
            centre = jnp.sum(attention * dprob, -1, keepdims=True)
            ds = (attention * (dprob - centre) * scaling).astype(BF16)
            attended[h, rows, :] = nn(attention_low, values).astype(BF16)
            dquery[h, rows, :] = nn(ds, keys).astype(BF16)
            for full, piece in ((prob, attention_low), (dscore, ds)):
                full[rows, 0:ROWS] = piece[:, 0:ROWS]
                for n in range(len(OFFSETS)):
                    part = piece[:, ROWS + n * TILE : ROWS + (n + 1) * TILE]
                    for s in range(2):
                        at = ROWS + (2 * n + s) * TILE
                        keep = jnp.where(pick[t][n] == s, 1.0, 0.0).astype(BF16)
                        full[rows, at : at + TILE] = part * keep

            if t == 2:

                @pl.when(h >= 1)
                def _():
                    add_pair(h - 1)

        at = pl.multiple_of(h * HW, HW)
        dk = nn(q_t[h], dscore[...]).astype(BF16)
        dv = nn(ga_t[h], prob[...]).astype(BF16)
        dkv_t[pl.ds(at, HW), :] = dk
        dkv_t[pl.ds(pl.multiple_of(D + h * HW, HW), HW), :] = dv
        local[h, :, 0:HW] = nn(normed_t[:, 0:ROWS], dquery[h]).astype(BF16)
        both = jnp.concatenate([dk, dv], 0)
        local[h, :, HW : 3 * HW] = nt(normed_t[...], both).astype(BF16)
        outer = tn(attended[h], c_ref[0]).astype(BF16)
        for r in range(D // HW):
            local[h, r * HW : (r + 1) * HW, 3 * HW :] = outer[:, r * HW : (r + 1) * HW]
        start(to_pair(h))
        return carry

    lax.fori_loop(0, HEADS, head, 0)

    def give_back(oi):
        at = ROWS + oi * HALO
        back_out[oi] = tt(dkv_t[:, at : at + HALO], w_ref[:, D:]).astype(BF16)

    def own_grad():
        total = tt(dkv_t[:, 0:ROWS], w_ref[:, D:])
        for h in range(HEADS):
            total = total + nt(dquery[h], w_ref[:, h * HW : (h + 1) * HW])
        return total

    def finish_features(grad):
        for oi in range(len(OFFSETS)):
            back_copy(oi).wait_recv()
        for r in range(LOCAL):
            rows = slice(r * TILE, (r + 1) * TILE)
            total = grad[rows]
            for oi in range(len(OFFSETS)):
                for s in range(2):
                    came = back_in[oi, s * TILE : (s + 1) * TILE, :].astype(F32)
                    total = total + jnp.where(named[oi][s] == r, came, 0.0)
            wide, inverse = normalise(x_ref[0, rows, :])
            normed = wide * inverse
            mean = jnp.mean(total * normed, -1, keepdims=True)
            result = c_ref[0, rows, :].astype(F32) + inverse * (total - normed * mean)
            gf_ref[0, rows, :] = result.astype(BF16)
        features_copy.start()

    def out_copy(index, owner, row):
        piece = (owned(lax.rem(owner - index + 2 * group, group)), rows_at(row, HALF), slice(None))
        return pltpu.make_async_copy(res.at[piece], out_ref.at[piece], out_sem.at[index])

    features_copy = pltpu.make_async_copy(gf_ref, gf_hbm, in_sem.at[6])
    give_back(0)
    give_back(3)
    add_pair(HEADS - 1)
    give_back(1)
    give_back(2)
    for h in range(HEADS):
        add_first(h)
    start(scatter_second())
    grad = own_grad()
    add_second()
    for oi in (0, 3, 1, 2):
        back_copy(oi).start()
    add_z()
    arrive(gather_z())
    start(gather_second())
    start(gather_first(0))
    for j in range(1, group):
        arrive(gather_second()[j - 1 : j])
        start(gather_first(j))
    finish_features(grad)
    for i in range(group):
        arrive(gather_first(i))
        start(gather_pair(i))
        out_copy(i, m2, half_at).start()
    for i in range(group):
        arrive(gather_pair(i))
        out_copy(group + i, m1, HALF - half_at).start()
    for oi in range(len(OFFSETS)):
        halo_copy(oi).wait_send()
        back_copy(oi).wait_send()

    def settle(h, carry):
        for copy in to_pair(h) + scatter_first(h):
            copy.wait_send()
        return carry

    lax.fori_loop(0, HEADS, settle, 0)
    for copy in scatter_second() + scatter_z() + gather_z() + gather_second():
        copy.wait_send()
    for i in range(group):
        for copy in gather_first(i) + gather_pair(i):
            copy.wait_send()
    for i in range(group):
        out_copy(i, m2, half_at).wait()
        out_copy(group + i, m1, HALF - half_at).wait()
    features_copy.wait()


def reduction_counts(group, nz):
    n1 = group - 1
    return [HEADS, HEADS * n1, n1, nz - 1, nz - 1, n1, group * n1, group]


def split_last(rows, count):
    down = min(count, rows // 16)
    return down, count // down


def finish(factor, chunks, features, qkv, out, grad_features):
    for h in range(HEADS):
        for part in range(3):
            piece = chunks[h, :, part * HW : (part + 1) * HW]
            at = part * D + h * HW
            qkv[:, at : at + HW] = piece.astype(F32) * factor
        column = pl.ds(pl.multiple_of(pl.program_id(0) * HW, HW), HW)
        out[h * HW : (h + 1) * HW, column] = chunks[h, :, 3 * HW :].astype(F32) * factor
    grad_features[...] = features[...]


def on_device(dims, features, cotangent, weight_qkv, weight_out, key_tiles, tile_valid):
    patches, nz, ny, nx = dims
    group = nx
    piece1 = HALF // group
    piece2 = HEADS // group * piece1
    down, across = split_last(piece2, nz)
    n_sem = sum(reduction_counts(group, nz))
    n_off = len(OFFSETS)
    grad_features, gathered = pl.pallas_call(
        functools.partial(kernel, dims),
        out_shape=(
            jax.ShapeDtypeStruct((1, ROWS, D), BF16),
            jax.ShapeDtypeStruct((HEADS, D, D), BF16),
        ),
        in_specs=[pl.BlockSpec(memory_space=pltpu.HBM)] * 6,
        out_specs=(pl.BlockSpec(memory_space=pl.ANY), pl.BlockSpec(memory_space=pl.ANY)),
        scratch_shapes=[
            pltpu.SMEM(key_tiles.shape[::-1], jnp.int32),
            pltpu.SMEM(tile_valid.shape[::-1], jnp.int32),
            pltpu.VMEM((1, ROWS, D), BF16),
            pltpu.VMEM((1, ROWS, D), BF16),
            pltpu.VMEM((1, ROWS, D), BF16),
            pltpu.VMEM((D, 3 * D), BF16),
            pltpu.VMEM((D, D), BF16),
            pltpu.VMEM((n_off, HALO, D), BF16),
            pltpu.VMEM((n_off, HALO, D), BF16),
            pltpu.VMEM((D, ALL), BF16),
            pltpu.VMEM((HEADS, ROWS, HW), BF16),
            pltpu.VMEM((HEADS, ALL, HW), BF16),
            pltpu.VMEM((HEADS, ALL, HW), BF16),
            pltpu.VMEM((HEADS, ROWS, HW), BF16),
            pltpu.VMEM((HEADS, HW, ROWS), BF16),
            pltpu.VMEM((HEADS, HW, ROWS), BF16),
            pltpu.VMEM((LOCAL, 8, 2 * ROWS), F32),
            pltpu.VMEM((HEADS, ROWS, ROWS), F32),
            pltpu.VMEM((HEADS, ROWS, ROWS), F32),
            pltpu.VMEM((ROWS, ALL), BF16),
            pltpu.VMEM((ROWS, ALL), BF16),
            pltpu.VMEM((HEADS, ROWS, HW), BF16),
            pltpu.VMEM((HEADS, ROWS, HW), BF16),
            pltpu.VMEM((2 * D, ALL), BF16),
            pltpu.VMEM((n_off, HALO, D), BF16),
            pltpu.VMEM((n_off, HALO, D), BF16),
            pltpu.VMEM((HEADS, D, D), BF16),
            pltpu.VMEM((HEADS, HALF, D), BF16),
            pltpu.VMEM((HEADS, HALF, D), BF16),
            pltpu.VMEM((HEADS, group - 1, piece1, D), BF16),
            pltpu.VMEM((HEADS * piece1, D), BF16),
            pltpu.VMEM((group - 1, piece2, D), BF16),
            pltpu.VMEM((piece2, D), BF16),
            pltpu.VMEM((nz - 1, piece2 // down, D // across), BF16),
            pltpu.VMEM((HEADS, D, D), BF16),
            pltpu.SemaphoreType.DMA((n_off,)),
            pltpu.SemaphoreType.DMA((n_off,)),
            pltpu.SemaphoreType.DMA((n_off,)),
            pltpu.SemaphoreType.DMA((n_off,)),
            pltpu.SemaphoreType.DMA((n_sem,)),
            pltpu.SemaphoreType.DMA((n_sem,)),
            pltpu.SemaphoreType.DMA((2 * group,)),
            pltpu.SemaphoreType.DMA((7,)),
        ],
        compiler_params=pltpu.CompilerParams(
            collective_id=0, has_side_effects=True, vmem_limit_bytes=60 * 1024 * 1024
        ),
        cost_estimate=pl.CostEstimate(
            flops=8 * 10**9, bytes_accessed=8 * 2**20, transcendentals=2 * 2**20
        ),
        name="layer",
    )(key_tiles.T, tile_valid.T, features, cotangent, weight_qkv, weight_out)
    factor = float(patches * nx * ROWS) ** (-0.5)
    grad_qkv, grad_out, grad_features = pl.pallas_call(
        functools.partial(finish, factor),
        grid=(D // HW,),
        out_shape=(
            jax.ShapeDtypeStruct((D, 3 * D), F32),
            jax.ShapeDtypeStruct((D, D), F32),
            jax.ShapeDtypeStruct((1, ROWS, D), BF16),
        ),
        in_specs=[
            pl.BlockSpec((HEADS, HW, D), lambda r: (0, r, 0)),
            pl.BlockSpec((1, HW, D), lambda r: (0, r, 0)),
        ],
        out_specs=(
            pl.BlockSpec((HW, 3 * D), lambda r: (r, 0)),
            pl.BlockSpec((D, D), lambda r: (0, 0)),
            pl.BlockSpec((1, HW, D), lambda r: (0, r, 0)),
        ),
        name="finish",
    )(gathered, grad_features)
    return grad_features, grad_qkv, grad_out


def solution(mesh):
    patches = mesh.shape["patch"]
    dims = (patches, patches // (2 * CHIPS_Y), CHIPS_Y, mesh.shape["sample"])
    placed = (P("sample", "patch", None), P("sample", "patch", None), P(), P(), P(), P())
    return jax.shard_map(
        functools.partial(on_device, dims),
        mesh=mesh,
        in_specs=placed,
        out_specs=(P("sample", "patch", None), P(), P()),
        check_vma=False,
    )
```

```python
import functools

import jax
import jax.numpy as jnp
from jax import lax
from jax.experimental import pallas as pl
from jax.experimental.pallas import tpu as pltpu
from jax.sharding import PartitionSpec as P

HEADS = 4
TILE = 128
LOCAL = 4
REACH = 2
OFFSETS = [-2, -1, 1, 2]
CHIPS_Y = 4
EPS = 1e-06
MESH = pl.DeviceIdType.MESH
F32 = jnp.float32
BF16 = jnp.bfloat16
LOG2E = 1.4426950408889634
ROWS = LOCAL * TILE
HALO = 2 * TILE
ALL = ROWS + len(OFFSETS) * HALO
D = 512
HW = D // HEADS
HALF = D // 2


def nn(a, b):
    return lax.dot_general(a, b, (((1,), (0,)), ((), ())), preferred_element_type=F32)


def nt(a, b):
    return lax.dot_general(a, b, (((1,), (1,)), ((), ())), preferred_element_type=F32)


def tt(a, b):
    return lax.dot_general(a, b, (((0,), (1,)), ((), ())), preferred_element_type=F32)


def tn(a, b):
    return lax.dot_general(a, b, (((0,), (0,)), ((), ())), preferred_element_type=F32)


def normalise(rows):
    wide = rows.astype(F32)
    inverse = lax.rsqrt(jnp.mean(wide * wide, -1, keepdims=True) + EPS)
    return wide, inverse


def kernel(
    dims,
    kt_hbm,
    tv_hbm,
    x_hbm,
    c_hbm,
    w_hbm,
    wo_hbm,
    gf_hbm,
    out_ref,
    kt,
    tv,
    gf_ref,
    x_ref,
    c_ref,
    w_ref,
    wo_ref,
    stage,
    halo,
    normed_t,
    q,
    k,
    v,
    ga,
    q_t,
    ga_t,
    bias,
    own_scores,
    own_dprob,
    prob,
    dscore,
    attended,
    dquery,
    dkv_t,
    back_out,
    back_in,
    local,
    got0,
    sum0,
    got1,
    sum1,
    got2,
    sum2,
    got3,
    res,
    halo_send,
    halo_recv,
    back_send,
    back_recv,
    red_send,
    red_recv,
    out_sem,
    in_sem,
):
    patches, nz, ny, nx = dims
    p = lax.axis_index("patch")
    sx = lax.axis_index("sample")
    core = lax.rem(p, 2)
    y = lax.rem(lax.div(p, 2), ny)
    z = lax.div(p, 2 * ny)

    def patch_at(zz, yy):
        return (zz * ny + yy) * 2 + core

    def first(j):
        return (
            patch_at(z, lax.rem(y + j * core, ny)),
            lax.rem(sx + j * (1 - core), nx),
        )

    def second(j):
        return (
            patch_at(z, lax.rem(y + j * (1 - core), ny)),
            lax.rem(sx + j * core, nx),
        )

    def along_z(j):
        return (patch_at(lax.rem(z + j, nz), y), sx)

    pair = (p + 1 - 2 * core, sx)
    m1 = sx * (1 - core) + y * core
    m2 = sx * core + y * (1 - core)
    group = nx

    loads = [
        pltpu.make_async_copy(src, dst, in_sem.at[i])
        for i, (src, dst) in enumerate(
            (
                (x_hbm, x_ref),
                (w_hbm, w_ref),
                (c_hbm, c_ref),
                (wo_hbm, wo_ref),
                (kt_hbm, kt),
                (tv_hbm, tv),
            )
        )
    ]
    for i in (4, 0, 5, 1, 2, 3):
        loads[i].start()

    barrier = pltpu.get_barrier_semaphore()
    greeted = (
        [(lax.rem(p + o + patches, patches), sx) for o in OFFSETS]
        + [pair]
        + [first(j) for j in range(1, group)]
        + [second(j) for j in range(1, group)]
        + [along_z(j) for j in range(1, nz)]
    )
    for device in greeted:
        pl.semaphore_signal(barrier, inc=1, device_id=device, device_id_type=MESH)

    loads[0].wait()
    loads[4].wait()
    named = []
    for oi, o in enumerate(OFFSETS):
        row = lax.rem(p - o + patches, patches) * LOCAL
        one = kt[LOCAL + oi, row]
        two = one
        for r in range(1, LOCAL):
            entry = kt[LOCAL + oi, row + r]
            two = jnp.where(entry != one, entry, two)
        named.append((one - p * LOCAL, two - p * LOCAL))
        for s in range(2):
            tile = x_ref[0, 0:TILE, :]
            for r in range(1, LOCAL):
                tile = jnp.where(named[oi][s] == r, x_ref[0, r * TILE : (r + 1) * TILE, :], tile)
            stage[oi, s * TILE : (s + 1) * TILE, :] = tile

    pl.semaphore_wait(barrier, len(greeted))

    def halo_copy(oi, o=None):
        o = OFFSETS[oi] if o is None else o
        return pltpu.make_async_remote_copy(
            src_ref=stage.at[oi],
            dst_ref=halo.at[oi],
            send_sem=halo_send.at[oi],
            recv_sem=halo_recv.at[oi],
            device_id=(lax.rem(p - o + patches, patches), sx),
            device_id_type=MESH,
        )

    def back_copy(oi):
        return pltpu.make_async_remote_copy(
            src_ref=back_out.at[oi],
            dst_ref=back_in.at[oi],
            send_sem=back_send.at[oi],
            recv_sem=back_recv.at[oi],
            device_id=(lax.rem(p + OFFSETS[oi] + patches, patches), sx),
            device_id_type=MESH,
        )

    for oi in (0, 3, 1, 2):
        halo_copy(oi).start()

    loads[5].wait()
    base = p * LOCAL
    pick = []
    for t in range(LOCAL):
        pick.append(
            [
                jnp.where(kt[LOCAL + n, base + t] != kt[LOCAL + n, base], 1, 0)
                for n in range(len(OFFSETS))
            ]
        )
        for r in range(LOCAL):
            flag = jnp.int32(0)
            for j in range(LOCAL):
                flag = flag + jnp.where(kt[j, base + t] == base + r, tv[j, base + t], 0)
            low = jnp.where(flag > 0, jnp.float32(0.0), jnp.float32(-1e30))
            bias[t, :, r * TILE : (r + 1) * TILE] = jnp.full((8, TILE), low, F32)
        for n in range(len(OFFSETS)):
            flag = tv[LOCAL + n, base + t]
            low = jnp.where(flag > 0, jnp.float32(0.0), jnp.float32(-1e30))
            bias[t, :, ROWS + n * TILE : ROWS + (n + 1) * TILE] = jnp.full((8, TILE), low, F32)

    loads[1].wait()
    wide, inverse = normalise(x_ref[0])
    low = (wide * inverse).astype(BF16)
    normed_t[:, 0:ROWS] = low.T
    for part, target in ((0, q), (1, k), (2, v)):
        for half in range(2):
            at = part * D + half * 2 * HW
            got = nn(low, w_ref[:, at : at + 2 * HW]).astype(BF16)
            for i in range(2):
                piece = got[:, i * HW : (i + 1) * HW]
                target[half * 2 + i, 0:ROWS, :] = piece
                if part == 0:
                    q_t[half * 2 + i] = piece.T
    loads[2].wait()
    loads[3].wait()
    for half in range(2):
        at = half * 2 * HW
        got = nt(c_ref[0], wo_ref[at : at + 2 * HW, :]).astype(BF16)
        for i in range(2):
            piece = got[:, i * HW : (i + 1) * HW]
            ga[half * 2 + i] = piece
            ga_t[half * 2 + i] = piece.T

    for h in range(HEADS):
        own_scores[h] = nt(q[h], k[h, 0:ROWS, :])
        own_dprob[h] = nt(ga[h], v[h, 0:ROWS, :])

    for oi, o in ((2 - core, 1 - 2 * core), (1 + core, 2 * core - 1), (0, -2), (3, 2)):
        halo_copy(oi, o).wait_recv()
        wide, inverse = normalise(halo[oi])
        low = (wide * inverse).astype(BF16)
        at_row = pl.ds(pl.multiple_of(ROWS + oi * HALO, HALO), HALO)
        normed_t[:, at_row] = low.T
        for part, target in ((1, k), (2, v)):
            for half in range(2):
                at = part * D + half * 2 * HW
                got = nn(low, w_ref[:, at : at + 2 * HW]).astype(BF16)
                for i in range(2):
                    target[half * 2 + i, at_row, :] = got[:, i * HW : (i + 1) * HW]

    n1 = group - 1
    piece1 = HALF // group
    per_owner = HEADS // group
    piece2 = per_owner * piece1
    down, across = split_last(piece2, nz)
    piece3, width3 = piece2 // down, D // across
    half_at = core * HALF
    at1 = half_at + m1 * piece1
    counts = reduction_counts(group, nz)
    firsts = [sum(counts[:i]) for i in range(len(counts))]

    def rows_at(start, size):
        return pl.ds(pl.multiple_of(start, 16), size)

    def owned(owner):
        return pl.ds(owner * per_owner, per_owner)

    def last_piece(index):
        return (
            rows_at(lax.div(index, across) * piece3, piece3),
            pl.ds(pl.multiple_of(lax.rem(index, across) * width3, 128), width3),
        )

    def last_place(index):
        row = lax.div(index, across) * piece3
        head_at = m2 * per_owner + lax.div(row, piece1)
        rows = rows_at(at1 + lax.rem(row, piece1), piece3)
        return head_at, rows, last_piece(index)[1]

    def move(phase, i, src, dst, device):
        return pltpu.make_async_remote_copy(
            src_ref=src,
            dst_ref=dst,
            send_sem=red_send.at[firsts[phase] + i],
            recv_sem=red_recv.at[firsts[phase] + i],
            device_id=device,
            device_id_type=MESH,
        )

    def to_pair(h):
        src = local.at[h, rows_at((1 - core) * HALF, HALF), :]
        return [move(0, h, src, got0.at[h], pair)]

    def scatter_first(h):
        return [
            move(
                1,
                h * n1 + j - 1,
                sum0.at[h, rows_at(lax.rem(m1 + j, group) * piece1, piece1), :],
                got1.at[h, j - 1],
                first(j),
            )
            for j in range(1, group)
        ]

    def scatter_second():
        return [
            move(
                2,
                j - 1,
                sum1.at[rows_at(lax.rem(m2 + j, group) * piece2, piece2), :],
                got2.at[j - 1],
                second(j),
            )
            for j in range(1, group)
        ]

    def scatter_z():
        moves = []
        for j in range(1, nz):
            rows, columns = last_piece(lax.rem(z + j, nz))
            moves.append(move(3, j - 1, sum2.at[rows, columns], got3.at[j - 1], along_z(j)))
        return moves

    def gather_z():
        mine = res.at[last_place(z)]
        return [move(4, j - 1, mine, mine, along_z(j)) for j in range(1, nz)]

    def gather_second():
        mine = res.at[owned(m2), rows_at(at1, piece1), :]
        return [move(5, j - 1, mine, mine, second(j)) for j in range(1, group)]

    def gather_first(i):
        mine = res.at[owned(lax.rem(m2 - i + group, group)), rows_at(at1, piece1), :]
        return [move(6, i * n1 + j - 1, mine, mine, first(j)) for j in range(1, group)]

    def gather_pair(i):
        mine = res.at[owned(lax.rem(m2 - i + group, group)), rows_at(half_at, HALF), :]
        return [move(7, i, mine, mine, pair)]

    def start(copies):
        for copy in copies:
            copy.start()

    def arrive(copies):
        for copy in copies:
            copy.wait_recv()

    def add_pair(h):
        arrive(to_pair(h))
        mine = local[h, rows_at(half_at, HALF), :].astype(F32)
        sum0[h] = (mine + got0[h].astype(F32)).astype(BF16)
        start(scatter_first(h))

    def add_first(h):
        arrive(scatter_first(h))
        total = sum0[h, rows_at(m1 * piece1, piece1), :].astype(F32)
        for j in range(n1):
            total = total + got1[h, j].astype(F32)
        sum1[h * piece1 : (h + 1) * piece1, :] = total.astype(BF16)

    def add_second():
        arrive(scatter_second())
        total = sum1[rows_at(m2 * piece2, piece2), :].astype(F32)
        for j in range(n1):
            total = total + got2[j].astype(F32)
        sum2[...] = total.astype(BF16)
        start(scatter_z())

    def add_z():
        arrive(scatter_z())
        total = sum2[last_piece(z)].astype(F32)
        for j in range(nz - 1):
            total = total + got3[j].astype(F32)
        res[last_place(z)] = total.astype(BF16)
        start(gather_z())

    scaling = HW ** (-0.5)

    def head(h, carry):
        for t in range(LOCAL):
            rows = slice(t * TILE, (t + 1) * TILE)

            def chosen(ref):
                parts = [ref[h, 0:ROWS, :]]
                for n in range(len(OFFSETS)):
                    at = ROWS + n * HALO
                    near = ref[h, at : at + TILE, :]
                    far = ref[h, at + TILE : at + HALO, :]
                    parts.append(jnp.where(pick[t][n] == 0, near, far))
                return jnp.concatenate(parts, 0)

            keys = chosen(k)
            values = chosen(v)
            scores = jnp.concatenate(
                [own_scores[h, rows, :], nt(q[h, rows, :], keys[ROWS:])], 1
            )
            scores = scores + bias[t, 0:1, :]
            highest = jnp.max(scores, -1, keepdims=True)
            expanded = jnp.exp2((scores - highest) * (scaling * LOG2E))
            attention = expanded * (1.0 / jnp.sum(expanded, -1, keepdims=True))
            attention_low = attention.astype(BF16)
            dprob = jnp.concatenate(
                [own_dprob[h, rows, :], nt(ga[h, rows, :], values[ROWS:])], 1
            )
            centre = jnp.sum(attention * dprob, -1, keepdims=True)
            ds = (attention * (dprob - centre) * scaling).astype(BF16)
            attended[h, rows, :] = nn(attention_low, values).astype(BF16)
            dquery[h, rows, :] = nn(ds, keys).astype(BF16)
            for full, piece in ((prob, attention_low), (dscore, ds)):
                full[rows, 0:ROWS] = piece[:, 0:ROWS]
                for n in range(len(OFFSETS)):
                    part = piece[:, ROWS + n * TILE : ROWS + (n + 1) * TILE]
                    for s in range(2):
                        at = ROWS + (2 * n + s) * TILE
                        keep = jnp.where(pick[t][n] == s, 1.0, 0.0).astype(BF16)
                        full[rows, at : at + TILE] = part * keep

            if t == 2:

                @pl.when(h >= 1)
                def _():
                    add_pair(h - 1)

        at = pl.multiple_of(h * HW, HW)
        dk = nn(q_t[h], dscore[...]).astype(BF16)
        dv = nn(ga_t[h], prob[...]).astype(BF16)
        dkv_t[pl.ds(at, HW), :] = dk
        dkv_t[pl.ds(pl.multiple_of(D + h * HW, HW), HW), :] = dv
        local[h, :, 0:HW] = nn(normed_t[:, 0:ROWS], dquery[h]).astype(BF16)
        both = jnp.concatenate([dk, dv], 0)
        local[h, :, HW : 3 * HW] = nt(normed_t[...], both).astype(BF16)
        outer = tn(attended[h], c_ref[0]).astype(BF16)
        for r in range(D // HW):
            local[h, r * HW : (r + 1) * HW, 3 * HW :] = outer[:, r * HW : (r + 1) * HW]
        start(to_pair(h))
        return carry

    lax.fori_loop(0, HEADS, head, 0)

    def give_back(oi):
        at = ROWS + oi * HALO
        back_out[oi] = tt(dkv_t[:, at : at + HALO], w_ref[:, D:]).astype(BF16)

    def own_grad():
        total = tt(dkv_t[:, 0:ROWS], w_ref[:, D:])
        for h in range(HEADS):
            total = total + nt(dquery[h], w_ref[:, h * HW : (h + 1) * HW])
        return total

    def finish_features(grad):
        for oi in range(len(OFFSETS)):
            back_copy(oi).wait_recv()
        for r in range(LOCAL):
            rows = slice(r * TILE, (r + 1) * TILE)
            total = grad[rows]
            for oi in range(len(OFFSETS)):
                for s in range(2):
                    came = back_in[oi, s * TILE : (s + 1) * TILE, :].astype(F32)
                    total = total + jnp.where(named[oi][s] == r, came, 0.0)
            wide, inverse = normalise(x_ref[0, rows, :])
            normed = wide * inverse
            mean = jnp.mean(total * normed, -1, keepdims=True)
            result = c_ref[0, rows, :].astype(F32) + inverse * (total - normed * mean)
            gf_ref[0, rows, :] = result.astype(BF16)
        features_copy.start()

    def out_copy(index, owner, row):
        piece = (owned(lax.rem(owner - index + 2 * group, group)), rows_at(row, HALF), slice(None))
        return pltpu.make_async_copy(res.at[piece], out_ref.at[piece], out_sem.at[index])

    features_copy = pltpu.make_async_copy(gf_ref, gf_hbm, in_sem.at[6])
    give_back(0)
    add_pair(HEADS - 1)
    give_back(1)
    give_back(2)
    for h in range(HEADS):
        add_first(h)
    start(scatter_second())
    give_back(3)
    add_second()
    for oi in (0, 3, 1, 2):
        back_copy(oi).start()
    add_z()
    arrive(gather_z())
    start(gather_second())
    start(gather_first(0))
    for j in range(1, group):
        arrive(gather_second()[j - 1 : j])
        start(gather_first(j))
    grad = own_grad()
    for i in range(group):
        arrive(gather_first(i))
        start(gather_pair(i))
        out_copy(i, m2, half_at).start()
    finish_features(grad)
    for oi in range(len(OFFSETS)):
        halo_copy(oi).wait_send()
        back_copy(oi).wait_send()

    def settle(h, carry):
        for copy in to_pair(h) + scatter_first(h):
            copy.wait_send()
        return carry

    lax.fori_loop(0, HEADS, settle, 0)
    for copy in scatter_second() + scatter_z() + gather_z() + gather_second():
        copy.wait_send()
    for i in range(group):
        for copy in gather_first(i):
            copy.wait_send()
    for i in range(group):
        arrive(gather_pair(i))
        out_copy(group + i, m1, HALF - half_at).start()
    for i in range(group):
        for copy in gather_pair(i):
            copy.wait_send()
        out_copy(i, m2, half_at).wait()
        out_copy(group + i, m1, HALF - half_at).wait()
    features_copy.wait()


def reduction_counts(group, nz):
    n1 = group - 1
    return [HEADS, HEADS * n1, n1, nz - 1, nz - 1, n1, group * n1, group]


def split_last(rows, count):
    down = min(count, rows // 16)
    return down, count // down


def finish(factor, chunks, features, qkv, out, grad_features, low, wide, wide_out, held, sem_in, sem_out):
    taken = pltpu.make_async_copy(features, held, sem_in.at[LOCAL])
    passed = pltpu.make_async_copy(held, grad_features, sem_out.at[LOCAL + 1])
    loads = []
    for r in range(LOCAL):
        rows = pl.ds(r * HW, HW)
        loads.append(pltpu.make_async_copy(chunks.at[:, rows, :], low.at[r], sem_in.at[r]))
        loads[r].start()
    taken.start()
    stores = []
    for r in range(LOCAL):
        loads[r].wait()
        for h in range(HEADS):
            for part in range(3):
                piece = low[r, h, :, part * HW : (part + 1) * HW]
                at = part * D + h * HW
                wide[r, :, at : at + HW] = piece.astype(F32) * factor
            piece = low[r, h, :, 3 * HW :].astype(F32) * factor
            wide_out[h * HW : (h + 1) * HW, r * HW : (r + 1) * HW] = piece
        stores.append(
            pltpu.make_async_copy(wide.at[r], qkv.at[pl.ds(r * HW, HW), :], sem_out.at[r])
        )
        stores[r].start()
    stores.append(pltpu.make_async_copy(wide_out, out, sem_out.at[LOCAL]))
    stores[LOCAL].start()
    taken.wait()
    passed.start()
    for store in stores:
        store.wait()
    passed.wait()


def on_device(dims, features, cotangent, weight_qkv, weight_out, key_tiles, tile_valid):
    patches, nz, ny, nx = dims
    group = nx
    piece1 = HALF // group
    piece2 = HEADS // group * piece1
    down, across = split_last(piece2, nz)
    n_sem = sum(reduction_counts(group, nz))
    n_off = len(OFFSETS)
    grad_features, gathered = pl.pallas_call(
        functools.partial(kernel, dims),
        out_shape=(
            jax.ShapeDtypeStruct((1, ROWS, D), BF16),
            jax.ShapeDtypeStruct((HEADS, D, D), BF16),
        ),
        in_specs=[pl.BlockSpec(memory_space=pltpu.HBM)] * 6,
        out_specs=(pl.BlockSpec(memory_space=pl.ANY), pl.BlockSpec(memory_space=pl.ANY)),
        scratch_shapes=[
            pltpu.SMEM(key_tiles.shape[::-1], jnp.int32),
            pltpu.SMEM(tile_valid.shape[::-1], jnp.int32),
            pltpu.VMEM((1, ROWS, D), BF16),
            pltpu.VMEM((1, ROWS, D), BF16),
            pltpu.VMEM((1, ROWS, D), BF16),
            pltpu.VMEM((D, 3 * D), BF16),
            pltpu.VMEM((D, D), BF16),
            pltpu.VMEM((n_off, HALO, D), BF16),
            pltpu.VMEM((n_off, HALO, D), BF16),
            pltpu.VMEM((D, ALL), BF16),
            pltpu.VMEM((HEADS, ROWS, HW), BF16),
            pltpu.VMEM((HEADS, ALL, HW), BF16),
            pltpu.VMEM((HEADS, ALL, HW), BF16),
            pltpu.VMEM((HEADS, ROWS, HW), BF16),
            pltpu.VMEM((HEADS, HW, ROWS), BF16),
            pltpu.VMEM((HEADS, HW, ROWS), BF16),
            pltpu.VMEM((LOCAL, 8, 2 * ROWS), F32),
            pltpu.VMEM((HEADS, ROWS, ROWS), F32),
            pltpu.VMEM((HEADS, ROWS, ROWS), F32),
            pltpu.VMEM((ROWS, ALL), BF16),
            pltpu.VMEM((ROWS, ALL), BF16),
            pltpu.VMEM((HEADS, ROWS, HW), BF16),
            pltpu.VMEM((HEADS, ROWS, HW), BF16),
            pltpu.VMEM((2 * D, ALL), BF16),
            pltpu.VMEM((n_off, HALO, D), BF16),
            pltpu.VMEM((n_off, HALO, D), BF16),
            pltpu.VMEM((HEADS, D, D), BF16),
            pltpu.VMEM((HEADS, HALF, D), BF16),
            pltpu.VMEM((HEADS, HALF, D), BF16),
            pltpu.VMEM((HEADS, group - 1, piece1, D), BF16),
            pltpu.VMEM((HEADS * piece1, D), BF16),
            pltpu.VMEM((group - 1, piece2, D), BF16),
            pltpu.VMEM((piece2, D), BF16),
            pltpu.VMEM((nz - 1, piece2 // down, D // across), BF16),
            pltpu.VMEM((HEADS, D, D), BF16),
            pltpu.SemaphoreType.DMA((n_off,)),
            pltpu.SemaphoreType.DMA((n_off,)),
            pltpu.SemaphoreType.DMA((n_off,)),
            pltpu.SemaphoreType.DMA((n_off,)),
            pltpu.SemaphoreType.DMA((n_sem,)),
            pltpu.SemaphoreType.DMA((n_sem,)),
            pltpu.SemaphoreType.DMA((2 * group,)),
            pltpu.SemaphoreType.DMA((7,)),
        ],
        compiler_params=pltpu.CompilerParams(
            collective_id=0, has_side_effects=True, vmem_limit_bytes=60 * 1024 * 1024
        ),
        cost_estimate=pl.CostEstimate(
            flops=8 * 10**9, bytes_accessed=8 * 2**20, transcendentals=2 * 2**20
        ),
        name="layer",
    )(key_tiles.T, tile_valid.T, features, cotangent, weight_qkv, weight_out)
    factor = float(patches * nx * ROWS) ** (-0.5)
    grad_qkv, grad_out, grad_features = pl.pallas_call(
        functools.partial(finish, factor),
        out_shape=(
            jax.ShapeDtypeStruct((D, 3 * D), F32),
            jax.ShapeDtypeStruct((D, D), F32),
            jax.ShapeDtypeStruct((1, ROWS, D), BF16),
        ),
        in_specs=[pl.BlockSpec(memory_space=pl.ANY)] * 2,
        out_specs=(pl.BlockSpec(memory_space=pl.ANY),) * 3,
        scratch_shapes=[
            pltpu.VMEM((LOCAL, HEADS, HW, D), BF16),
            pltpu.VMEM((LOCAL, HW, 3 * D), F32),
            pltpu.VMEM((D, D), F32),
            pltpu.VMEM((1, ROWS, D), BF16),
            pltpu.SemaphoreType.DMA((LOCAL + 1,)),
            pltpu.SemaphoreType.DMA((LOCAL + 2,)),
        ],
        compiler_params=pltpu.CompilerParams(vmem_limit_bytes=60 * 1024 * 1024),
        name="finish",
    )(gathered, grad_features)
    return grad_features, grad_qkv, grad_out


def solution(mesh):
    patches = mesh.shape["patch"]
    dims = (patches, patches // (2 * CHIPS_Y), CHIPS_Y, mesh.shape["sample"])
    placed = (P("sample", "patch", None), P("sample", "patch", None), P(), P(), P(), P())
    return jax.shard_map(
        functools.partial(on_device, dims),
        mesh=mesh,
        in_specs=placed,
        out_specs=(P("sample", "patch", None), P(), P()),
        check_vma=False,
    )
```
